256 devices in a mesh: row: 8 (over z_lo, core), lab: 32 (over y, x, z_hi).
Axes of the slice: x: 4, y: 4, z: 8 (z_hi: 2, z_lo: 4; z = z_hi * 4 + z_lo), core: 2. Of those that a mesh axis runs over, the one named last changes fastest.
Arguments:
- scores: bfloat16 [65536, 8192], P('row', 'lab'), may hold values from -8 to 8
- targets: int32 [65536, 8192], P('row', 'lab'), may hold values 0 or 1
- signs: int32 [8192, 16], P('lab'), may hold values from 0 to 1
- bins: int32 [65536, 512], P('row', 'lab'), may hold values from 0 to 255
- leaves: int32 [65536], P('row'), may hold values from 0 to 3
Outputs:
- histogram: float32 [256, 512, 68], P('row', 'lab')
The draws below stay inside these ranges and needn't reach their ends.
All inputs are finite; a program needn't handle non-finite values. No bound on the sum of `targets` on one device may be relied on, other than what follows from the above.
Results may differ from the reference program's by a relative error of at most 0.00091.
Values sent between devices are 32-bit elements; how exact they have to be, the bound alone decides.
No kernel may reach another device: no remote copies, remote signals or barrier semaphores. Data moves between devices by JAX's collectives and lax.ppermute only.
A program may use at most 64 MiB of HBM per device.

```python
import math
import jax
import jax.numpy as jnp
from jax import lax

L = 8192
F = 512
BINS = 256
K = 16
LEAVES = 4
ROWS = 65536


def touch_ends(result, stream_key, smallest, top_value):
    longest = result.shape.index(max(result.shape))
    spots = []
    for shift in (0, 1):
        where = [jax.random.randint(jax.random.fold_in(stream_key, axis), (), 0, length) for axis, length in enumerate(result.shape)]
        where[longest] = (where[longest] + shift) % result.shape[longest]
        spots.append(tuple(where))
    return result.at[spots[0]].set(smallest).at[spots[1]].set(top_value)


def shard_levels(own_key, extent, shards, low, largest):
    def one(axis_at, parts):
        steps = jax.random.uniform(jax.random.fold_in(jax.random.fold_in(own_key, 6), axis_at), (parts,), jnp.float32, low / len(shards), largest / len(shards))
        return jnp.repeat(jnp.exp(steps), extent[axis_at] // parts).reshape((-1,) + (1,) * (len(extent) - axis_at - 1))

    gain = one(*shards[0])
    for cut in shards[1:]:
        gain = gain * one(*cut)
    return gain


def centred(key, dims, deviation, reach, shards=(), kind=jnp.bfloat16):
    values = deviation * jax.random.normal(key, dims, jnp.float32)
    if shards:
        values = values * shard_levels(key, dims, shards, -0.22, 0.18)
    return jnp.clip(values, -reach, reach).astype(kind)


def setup_inputs(seed: int = 0) -> dict:
    splits = jax.random.split(jax.random.key(seed), 6)
    return {
        "scores": centred(splits[0], (ROWS, L), 2.0, 8.0, ((0, 8), (1, 32))),
        "targets": touch_ends((jax.random.randint(splits[1], (ROWS, L), 0, 4) < 1).astype(jnp.int32), jax.random.fold_in(splits[1], 1), 0, 1),
        "signs": touch_ends(jax.random.randint(splits[2], (L, K), 0, 2), jax.random.fold_in(splits[2], 1), 0, 1).astype(jnp.int32),
        "bins": touch_ends(jax.random.randint(splits[3], (ROWS, F), 0, BINS), jax.random.fold_in(splits[3], 1), 0, BINS - 1).astype(jnp.int32),
        "leaves": touch_ends(jax.random.randint(splits[4], (ROWS,), 0, LEAVES), jax.random.fold_in(splits[4], 1), 0, LEAVES - 1).astype(jnp.int32),
    }


def reference(scores, targets, signs, bins, leaves):
    sign_matrix = (2 * signs - 1).astype(jnp.float32)
    block_rows = min(4096, ROWS)

    def label_stats(pair):
        block_scores, block_targets = pair
        prob = jax.nn.sigmoid(block_scores.astype(jnp.float32))
        gradient = prob - block_targets.astype(jnp.float32)
        hessian = prob * (1.0 - prob)
        sketch = jnp.dot(gradient, sign_matrix, precision=lax.Precision.HIGHEST, preferred_element_type=jnp.float32) / math.sqrt(L)
        curvature = lax.optimization_barrier(jnp.sum(hessian, axis=1)) / L
        return jnp.concatenate([sketch, curvature[:, None]], axis=1)
    stats = lax.map(label_stats, (scores.reshape(ROWS // block_rows, block_rows, L), targets.reshape(ROWS // block_rows, block_rows, L)))
    stats = stats.reshape(ROWS, K + 1)
    leaf_onehot = (leaves[:, None] == jnp.arange(LEAVES, dtype=jnp.int32)[None, :]).astype(jnp.float32)
    weights = (leaf_onehot[:, :, None] * stats[:, None, :]).reshape(ROWS, LEAVES * (K + 1)).astype(jnp.bfloat16)
    wide = weights.astype(jnp.float32)

    def one_feature(column):
        return jax.ops.segment_sum(wide, column, num_segments=BINS)
    per_feature = lax.map(one_feature, bins.T)
    return jnp.transpose(per_feature, (1, 0, 2))
```

```python
import functools
import math

import jax
import jax.numpy as jnp
from jax import lax
from jax.experimental import pallas as pl
from jax.experimental.pallas import tpu as pltpu
from jax.sharding import Mesh, PartitionSpec as P

L = 8192
BINS = 256
K = 16
LEAVES = 4
ROWS = 8192
LABS = 256
FEATS = 16
SLAB = 512
LANES = 128
QUADS = SLAB // LANES
SLAB_ROWS = QUADS * (K + 1)
F8 = jnp.float8_e4m3fn
NT = (((1,), (1,)), ((), ()))
SKETCH_SCALES = (4.0, 64.0, 2.0**24, 2.0**29)
CURVE_SCALES = (1024.0, 2.0**14)
TERM_ROWS = LEAVES * K
W_ROWS = 288
OWN_BINS = 32


def sketch_kernel(chunk_ref, scores_ref, targets_ref, signs_ref, out_ref):
    del chunk_ref
    sign_matrix = (2 * signs_ref[...] - 1).astype(jnp.bfloat16)
    left = jnp.concatenate(
        [
            jnp.concatenate([sign_matrix, sign_matrix, jnp.zeros((K, LABS), jnp.bfloat16)], axis=1),
            jnp.concatenate(
                [jnp.zeros((K, 2 * LABS), jnp.bfloat16), jnp.ones((K, LABS), jnp.bfloat16)], axis=1
            ),
        ],
        axis=0,
    )
    prob = jax.nn.sigmoid(scores_ref[...].astype(jnp.float32))
    gradient = prob - targets_ref[...].astype(jnp.float32)
    hessian = prob * (1.0 - prob)
    hessian = hessian[:, :LANES] + hessian[:, LANES:]
    grad_high = gradient.astype(jnp.bfloat16)
    grad_low = (gradient - grad_high.astype(jnp.float32)).astype(jnp.bfloat16)
    hess_high = hessian.astype(jnp.bfloat16)
    hess_low = (hessian - hess_high.astype(jnp.float32)).astype(jnp.bfloat16)
    right = jnp.concatenate([grad_high, grad_low, hess_high, hess_low], axis=1)
    stats = lax.dot_general(left, right, NT, preferred_element_type=jnp.float32)
    for quad in range(QUADS):
        lanes = slice(quad * LANES, (quad + 1) * LANES)
        out_ref[0, quad * K : (quad + 1) * K, :] = stats[:K, lanes] * (1.0 / math.sqrt(L))
        out_ref[0, QUADS * K + quad : QUADS * K + quad + 1, :] = stats[K : K + 1, lanes] * (1.0 / L)


def sketch_call(chunk, scores, targets, signs_t):
    return pl.pallas_call(
        sketch_kernel,
        grid_spec=pltpu.PrefetchScalarGridSpec(
            num_scalar_prefetch=1,
            grid=(4,),
            in_specs=[
                pl.BlockSpec((SLAB, LABS), lambda i, c: (c[0] * 4 + i, 0)),
                pl.BlockSpec((SLAB, LABS), lambda i, c: (c[0] * 4 + i, 0)),
                pl.BlockSpec((K, LABS), lambda i, c: (0, 0)),
            ],
            out_specs=pl.BlockSpec((1, SLAB_ROWS, LANES), lambda i, c: (i, 0, 0)),
        ),
        out_shape=jax.ShapeDtypeStruct((4, SLAB_ROWS, LANES), jnp.float32),
        compiler_params=pltpu.CompilerParams(vmem_limit_bytes=16 << 20),
        cost_estimate=pl.CostEstimate(
            flops=2 * 4 * SLAB * 768 * 32, bytes_accessed=4 * SLAB * LABS * 6, transcendentals=4 * SLAB * LABS
        ),
        name="sketch",
    )(chunk, scores, targets, signs_t)


def split_terms(values, scales):
    terms = []
    for scale in scales:
        term = (values * scale).astype(F8).astype(jnp.float32)
        terms.append(term)
        values = values - term * (1.0 / scale)
    return terms


def weight_kernel(place_ref, s0, s1, s2, s3, leaves_ref, out_ref):
    leaf_iota = lax.broadcasted_iota(jnp.int32, (8, LANES), 0)
    zeros = jnp.zeros((K, LANES), jnp.float32)
    for kx, stats_ref in enumerate((s0, s1, s2, s3)):
        for ky in range(4):
            chunk = place_ref[kx] * 4 + place_ref[4 + ky]
            for quad in range(QUADS):
                leaf = leaves_ref[pl.ds(chunk * QUADS + quad, 1), :]
                sketch = stats_ref[ky, quad * K : (quad + 1) * K, :]
                curve = stats_ref[ky, QUADS * K + quad : QUADS * K + quad + 1, :]
                sketch = sketch.astype(jnp.bfloat16).astype(jnp.float32)
                curve = jnp.broadcast_to(curve, (8, LANES)).astype(jnp.bfloat16).astype(jnp.float32)
                masks = [jnp.broadcast_to(leaf == e, (K, LANES)) for e in range(LEAVES)]
                curve_mask = jnp.broadcast_to(leaf, (8, LANES)) == leaf_iota
                parts = [
                    jnp.where(mask, term, zeros)
                    for term in split_terms(sketch, SKETCH_SCALES)
                    for mask in masks
                ]
                parts += [jnp.where(curve_mask, term, 0.0) for term in split_terms(curve, CURVE_SCALES)]
                parts.append(jnp.zeros((W_ROWS - 4 * TERM_ROWS - 16, LANES), jnp.float32))
                lanes = pl.ds(pl.multiple_of(chunk * SLAB + quad * LANES, LANES), LANES)
                out_ref[:, lanes] = jnp.concatenate(parts, axis=0).astype(F8)


def weight_call(place, stats, leaves):
    return pl.pallas_call(
        weight_kernel,
        grid_spec=pltpu.PrefetchScalarGridSpec(
            num_scalar_prefetch=1,
            grid=(1,),
            in_specs=[pl.BlockSpec((4, SLAB_ROWS, LANES), lambda i, s: (0, 0, 0))] * 4
            + [pl.BlockSpec((ROWS // LANES, LANES), lambda i, s: (0, 0))],
            out_specs=pl.BlockSpec((W_ROWS, ROWS), lambda i, s: (0, 0)),
        ),
        out_shape=jax.ShapeDtypeStruct((W_ROWS, ROWS), F8),
        compiler_params=pltpu.CompilerParams(vmem_limit_bytes=24 << 20),
        cost_estimate=pl.CostEstimate(flops=20_000_000, bytes_accessed=4_000_000, transcendentals=0),
        name="weights",
    )(place, *stats, leaves)


def hist_kernel(base_ref, bins_ref, weights_ref, own_ref, other_ref):
    for which, out_ref in ((0, other_ref), (1, own_ref)):
        codes = bins_ref[...] - base_ref[which]
        codes = jnp.clip(codes, -1, OWN_BINS)
        pair = jnp.concatenate([codes, codes - 1], axis=0).astype(jnp.int8)
        one = jnp.ones(pair.shape, F8)
        zero = jnp.zeros(pair.shape, F8)
        onehot = jnp.concatenate(
            [jnp.where(pair == jnp.int8(b), one, zero) for b in range(0, OWN_BINS, 2)], axis=0
        )
        total = lax.dot_general(weights_ref[...], onehot, NT, preferred_element_type=jnp.float32)
        sketch = sum(
            total[t * TERM_ROWS : (t + 1) * TERM_ROWS] * (1.0 / scale)
            for t, scale in enumerate(SKETCH_SCALES)
        )
        curve = sum(
            total[4 * TERM_ROWS + 8 * t : 4 * TERM_ROWS + 8 * t + 8] * (1.0 / scale)
            for t, scale in enumerate(CURVE_SCALES)
        )
        out_ref[:TERM_ROWS, :] = sketch
        out_ref[TERM_ROWS:, :] = curve[:LEAVES]


def hist_call(base, bins_t, weights):
    cols = OWN_BINS * FEATS
    shape = jax.ShapeDtypeStruct((LEAVES * (K + 1), cols), jnp.float32)
    spec = pl.BlockSpec((LEAVES * (K + 1), cols), lambda i, s: (0, 0))
    return pl.pallas_call(
        hist_kernel,
        grid_spec=pltpu.PrefetchScalarGridSpec(
            num_scalar_prefetch=1,
            grid=(1,),
            in_specs=[
                pl.BlockSpec((FEATS, ROWS), lambda i, s: (0, 0)),
                pl.BlockSpec((W_ROWS, ROWS), lambda i, s: (0, 0)),
            ],
            out_specs=[spec, spec],
        ),
        out_shape=[shape, shape],
        compiler_params=pltpu.CompilerParams(vmem_limit_bytes=40 << 20),
        cost_estimate=pl.CostEstimate(
            flops=2 * 2 * cols * ROWS * W_ROWS, bytes_accessed=3_000_000, transcendentals=0
        ),
        name="hist",
    )(base, bins_t, weights)


def finish_kernel(a_ref, b_ref, c_ref, d_ref, out_ref):
    total = (a_ref[...] + b_ref[...]) + (c_ref[...] + d_ref[...])
    rows = []
    for e in range(LEAVES):
        rows.append(total[e * K : (e + 1) * K])
        rows.append(total[TERM_ROWS + e : TERM_ROWS + e + 1])
    total = jnp.concatenate(rows, axis=0)
    out_ref[...] = total.T.reshape(OWN_BINS, FEATS, LEAVES * (K + 1))


def finish_call(parts):
    return pl.pallas_call(
        finish_kernel,
        out_shape=jax.ShapeDtypeStruct((OWN_BINS, FEATS, LEAVES * (K + 1)), jnp.float32),
        name="finish",
    )(*parts)


def shift(value, axis, step, size):
    return lax.ppermute(value, axis, [(i, (i + step) % size) for i in range(size)])


def swap(value, axis, bit, size):
    return lax.ppermute(value, axis, [(i, i ^ bit) for i in range(size)])


def per_device(scores, targets, signs, bins, leaves):
    x = lax.axis_index("x")
    y = lax.axis_index("y")
    zl = lax.axis_index("zl")
    core = lax.axis_index("c")
    signs_t = signs.T
    bins_t = bins.T
    leaves2 = leaves.reshape(ROWS // LANES, LANES)

    arrived = []
    for k in (2, 1, 3, 0):
        chunk = ((x + k) % 4).astype(jnp.int32).reshape(1)
        part = sketch_call(chunk, scores, targets, signs_t)
        arrived.append(shift(part, "x", k, 4) if k else part)
    mine = (arrived[0] + arrived[1]) + (arrived[2] + arrived[3])
    arrived = [lax.dynamic_index_in_dim(mine, y, 0, keepdims=False)]
    for k in (2, 1, 3):
        arrived.append(shift(lax.dynamic_index_in_dim(mine, (y + k) % 4, 0, keepdims=False), "y", k, 4))
    mine = (arrived[0] + arrived[1]) + (arrived[2] + arrived[3])
    mine = mine + swap(mine, "zh", 1, 2)
    slabs = jnp.stack([mine] + [shift(mine, "y", k, 4) for k in (1, 2, 3)])
    blocks = [slabs] + [shift(slabs, "x", k, 4) for k in (1, 2, 3)]
    place = jnp.stack([(x - k) % 4 for k in range(4)] + [(y - k) % 4 for k in range(4)]).astype(jnp.int32)
    weights = weight_call(place, blocks, leaves2)

    parts = []
    for k in (3, 2, 1, 0):
        first = 2 * OWN_BINS * (zl ^ k)
        base = jnp.stack([first + OWN_BINS * (1 - core), first + OWN_BINS * core]).astype(jnp.int32)
        own, other = hist_call(base, bins_t, weights)
        part = own + swap(other, "c", 1, 2)
        parts.append(swap(part, "zl", k, 4) if k else part)
    return finish_call(parts)


def solution(mesh):
    fine = Mesh(mesh.devices.reshape(4, 2, 4, 4, 2), ("zl", "c", "y", "x", "zh"))
    row, lab = ("zl", "c"), ("y", "x", "zh")
    in_specs = (P(row, lab), P(row, lab), P(lab, None), P(row, lab), P(row))
    out_specs = P(row, lab, None)
    return jax.shard_map(
        per_device, mesh=fine, in_specs=in_specs, out_specs=out_specs, check_vma=False
    )
```

```python
import functools
import math

import jax
import jax.numpy as jnp
from jax import lax
from jax.experimental import pallas as pl
from jax.experimental.pallas import tpu as pltpu
from jax.sharding import Mesh, PartitionSpec as P

L = 8192
BINS = 256
K = 16
LEAVES = 4
ROWS = 8192
LABS = 256
FEATS = 16
SLAB = 512
LANES = 128
QUADS = SLAB // LANES
SLAB_ROWS = QUADS * (K + 1)
F8 = jnp.float8_e4m3fn
NT = (((1,), (1,)), ((), ()))
SKETCH_SCALES = (4.0, 64.0, 2.0**24, 2.0**29)
CURVE_SCALES = (1024.0, 2.0**14)
TERM_ROWS = LEAVES * K
W_ROWS = 288
OWN_BINS = 32
HIST_COST = 1000


def sketch_kernel(chunk_ref, scores_ref, targets_ref, signs_ref, out_ref):
    del chunk_ref
    sign_matrix = (2 * signs_ref[...] - 1).astype(jnp.bfloat16)
    left = jnp.concatenate(
        [
            jnp.concatenate([sign_matrix, sign_matrix, jnp.zeros((K, LABS), jnp.bfloat16)], axis=1),
            jnp.concatenate(
                [jnp.zeros((K, 2 * LABS), jnp.bfloat16), jnp.ones((K, LABS), jnp.bfloat16)], axis=1
            ),
        ],
        axis=0,
    )
    prob = jax.nn.sigmoid(scores_ref[...].astype(jnp.float32))
    gradient = prob - targets_ref[...].astype(jnp.float32)
    hessian = prob * (1.0 - prob)
    hessian = hessian[:, :LANES] + hessian[:, LANES:]
    grad_high = gradient.astype(jnp.bfloat16)
    grad_low = (gradient - grad_high.astype(jnp.float32)).astype(jnp.bfloat16)
    hess_high = hessian.astype(jnp.bfloat16)
    hess_low = (hessian - hess_high.astype(jnp.float32)).astype(jnp.bfloat16)
    right = jnp.concatenate([grad_high, grad_low, hess_high, hess_low], axis=1)
    stats = lax.dot_general(left, right, NT, preferred_element_type=jnp.float32)
    for quad in range(QUADS):
        lanes = slice(quad * LANES, (quad + 1) * LANES)
        out_ref[0, quad * K : (quad + 1) * K, :] = stats[:K, lanes] * (1.0 / math.sqrt(L))
        out_ref[0, QUADS * K + quad : QUADS * K + quad + 1, :] = stats[K : K + 1, lanes] * (1.0 / L)


def sketch_call(chunk, scores, targets, signs_t):
    return pl.pallas_call(
        sketch_kernel,
        grid_spec=pltpu.PrefetchScalarGridSpec(
            num_scalar_prefetch=1,
            grid=(4,),
            in_specs=[
                pl.BlockSpec((SLAB, LABS), lambda i, c: (c[0] * 4 + i, 0)),
                pl.BlockSpec((SLAB, LABS), lambda i, c: (c[0] * 4 + i, 0)),
                pl.BlockSpec((K, LABS), lambda i, c: (0, 0)),
            ],
            out_specs=pl.BlockSpec((1, SLAB_ROWS, LANES), lambda i, c: (i, 0, 0)),
        ),
        out_shape=jax.ShapeDtypeStruct((4, SLAB_ROWS, LANES), jnp.float32),
        compiler_params=pltpu.CompilerParams(vmem_limit_bytes=58 << 20),
        cost_estimate=pl.CostEstimate(
            flops=2 * 4 * SLAB * 768 * 32, bytes_accessed=4 * SLAB * LABS * 6, transcendentals=4 * SLAB * LABS
        ),
        name="sketch",
    )(chunk, scores, targets, signs_t)


def split_terms(values, scales):
    terms = []
    for scale in scales:
        term = (values * scale).astype(F8).astype(jnp.float32)
        terms.append(term)
        values = values - term * (1.0 / scale)
    return terms


def weight_kernel(place_ref, s0, s1, s2, s3, leaves_ref, out_ref):
    leaf_iota = lax.broadcasted_iota(jnp.int32, (8, LANES), 0)
    zeros = jnp.zeros((K, LANES), jnp.float32)
    for kx, stats_ref in enumerate((s0, s1, s2, s3)):
        for ky in range(4):
            chunk = place_ref[kx] * 4 + ky
            for quad in range(QUADS):
                leaf = leaves_ref[pl.ds(chunk * QUADS + quad, 1), :]
                sketch = stats_ref[ky, quad * K : (quad + 1) * K, :]
                curve = stats_ref[ky, QUADS * K + quad : QUADS * K + quad + 1, :]
                sketch = sketch.astype(jnp.bfloat16).astype(jnp.float32)
                curve = jnp.broadcast_to(curve, (8, LANES)).astype(jnp.bfloat16).astype(jnp.float32)
                masks = [jnp.broadcast_to(leaf == e, (K, LANES)) for e in range(LEAVES)]
                curve_mask = jnp.broadcast_to(leaf, (8, LANES)) == leaf_iota
                parts = [
                    jnp.where(mask, term, zeros)
                    for term in split_terms(sketch, SKETCH_SCALES)
                    for mask in masks
                ]
                parts += [jnp.where(curve_mask, term, 0.0) for term in split_terms(curve, CURVE_SCALES)]
                parts.append(jnp.zeros((W_ROWS - 4 * TERM_ROWS - 16, LANES), jnp.float32))
                lanes = pl.ds(pl.multiple_of(chunk * SLAB + quad * LANES, LANES), LANES)
                out_ref[:, lanes] = jnp.concatenate(parts, axis=0).astype(F8)


def weight_call(place, stats, leaves):
    return pl.pallas_call(
        weight_kernel,
        grid_spec=pltpu.PrefetchScalarGridSpec(
            num_scalar_prefetch=1,
            grid=(1,),
            in_specs=[pl.BlockSpec((4, SLAB_ROWS, LANES), lambda i, s: (0, 0, 0))] * 4
            + [pl.BlockSpec((ROWS // LANES, LANES), lambda i, s: (0, 0))],
            out_specs=pl.BlockSpec((W_ROWS, ROWS), lambda i, s: (0, 0)),
        ),
        out_shape=jax.ShapeDtypeStruct((W_ROWS, ROWS), F8),
        compiler_params=pltpu.CompilerParams(vmem_limit_bytes=24 << 20),
        cost_estimate=pl.CostEstimate(flops=20_000_000, bytes_accessed=4_000_000, transcendentals=0),
        name="weights",
    )(place, *stats, leaves)


def hist_kernel(base_ref, bins_ref, weights_ref, own_ref, other_ref):
    for which, out_ref in ((0, other_ref), (1, own_ref)):
        codes = bins_ref[...] - base_ref[which]
        codes = jnp.clip(codes, -1, OWN_BINS)
        pair = jnp.concatenate([codes, codes - 1], axis=0).astype(jnp.int8)
        one = jnp.ones(pair.shape, F8)
        zero = jnp.zeros(pair.shape, F8)
        onehot = jnp.concatenate(
            [jnp.where(pair == jnp.int8(b), one, zero) for b in range(0, OWN_BINS, 2)], axis=0
        )
        total = lax.dot_general(weights_ref[...], onehot, NT, preferred_element_type=jnp.float32)
        sketch = sum(
            total[t * TERM_ROWS : (t + 1) * TERM_ROWS] * (1.0 / scale)
            for t, scale in enumerate(SKETCH_SCALES)
        )
        curve = sum(
            total[4 * TERM_ROWS + 8 * t : 4 * TERM_ROWS + 8 * t + 8] * (1.0 / scale)
            for t, scale in enumerate(CURVE_SCALES)
        )
        out_ref[:TERM_ROWS, :] = sketch
        out_ref[TERM_ROWS:, :] = curve[:LEAVES]


def hist_call(base, bins_t, weights):
    cols = OWN_BINS * FEATS
    shape = jax.ShapeDtypeStruct((LEAVES * (K + 1), cols), jnp.float32)
    spec = pl.BlockSpec((LEAVES * (K + 1), cols), lambda i, s: (0, 0))
    return pl.pallas_call(
        hist_kernel,
        grid_spec=pltpu.PrefetchScalarGridSpec(
            num_scalar_prefetch=1,
            grid=(1,),
            in_specs=[
                pl.BlockSpec((FEATS, ROWS), lambda i, s: (0, 0)),
                pl.BlockSpec((W_ROWS, ROWS), lambda i, s: (0, 0)),
            ],
            out_specs=[spec, spec],
        ),
        out_shape=[shape, shape],
        compiler_params=pltpu.CompilerParams(vmem_limit_bytes=40 << 20),
        cost_estimate=pl.CostEstimate(
            flops=HIST_COST, bytes_accessed=1000, transcendentals=0
        ),
        name="hist",
    )(base, bins_t, weights)


def finish_kernel(a_ref, b_ref, c_ref, d_ref, out_ref):
    total = (a_ref[...] + b_ref[...]) + (c_ref[...] + d_ref[...])
    rows = []
    for e in range(LEAVES):
        rows.append(total[e * K : (e + 1) * K])
        rows.append(total[TERM_ROWS + e : TERM_ROWS + e + 1])
    total = jnp.concatenate(rows, axis=0)
    out_ref[...] = total.T.reshape(OWN_BINS, FEATS, LEAVES * (K + 1))


def finish_call(parts):
    return pl.pallas_call(
        finish_kernel,
        out_shape=jax.ShapeDtypeStruct((OWN_BINS, FEATS, LEAVES * (K + 1)), jnp.float32),
        compiler_params=pltpu.CompilerParams(vmem_limit_bytes=8 << 20),
        name="finish",
    )(*parts)


def swap(value, axis, bit, size):
    return lax.ppermute(value, axis, [(i, i ^ bit) for i in range(size)])


def per_device(scores, targets, signs, bins, leaves):
    x = lax.axis_index("x").astype(jnp.int32)
    zl = lax.axis_index("zl").astype(jnp.int32)
    core = lax.axis_index("c").astype(jnp.int32)
    signs_t = signs.T
    bins_t = bins.T
    leaves2 = leaves.reshape(ROWS // LANES, LANES)

    arrived = []
    for k in (2, 1, 3, 0):
        part = sketch_call((x ^ k).reshape(1), scores, targets, signs_t)
        arrived.append(swap(part, "x", k, 4) if k else part)
    mine = (arrived[0] + arrived[1]) + (arrived[2] + arrived[3])
    arrived = [swap(mine, "y", k, 4) for k in (2, 1, 3)]
    mine = (mine + arrived[0]) + (arrived[1] + arrived[2])
    mine = mine + swap(mine, "zh", 1, 2)
    blocks = [mine] + [swap(mine, "x", k, 4) for k in (1, 2, 3)]
    weights = weight_call(jnp.stack([x ^ k for k in range(4)]), blocks, leaves2)

    sums, parts = [], []
    for step, k in enumerate((3, 2, 1, 0)):
        first = 2 * OWN_BINS * (zl ^ k)
        base = jnp.stack([first + OWN_BINS * (1 - core), first + OWN_BINS * core])
        if step >= 2:
            base, sums[step - 2] = lax.optimization_barrier((base, sums[step - 2]))
            parts.append(swap(sums[step - 2], "zl", (3, 2)[step - 2], 4))
        own, other = hist_call(base, bins_t, weights)
        sums.append(own + swap(other, "c", 1, 2))
    parts += [swap(sums[2], "zl", 1, 4), sums[3]]
    return finish_call(parts)


def solution(mesh):
    fine = Mesh(mesh.devices.reshape(4, 2, 4, 4, 2), ("zl", "c", "y", "x", "zh"))
    row, lab = ("zl", "c"), ("y", "x", "zh")
    in_specs = (P(row, lab), P(row, lab), P(lab, None), P(row, lab), P(row))
    out_specs = P(row, lab, None)
    return jax.shard_map(
        per_device, mesh=fine, in_specs=in_specs, out_specs=out_specs, check_vma=False
    )
```

```python
import functools
import math

import jax
import jax.numpy as jnp
from jax import lax
from jax.experimental import pallas as pl
from jax.experimental.pallas import tpu as pltpu
from jax.sharding import Mesh, PartitionSpec as P

L = 8192
BINS = 256
K = 16
LEAVES = 4
ROWS = 8192
LABS = 256
FEATS = 16
SLAB = 512
LANES = 128
QUADS = SLAB // LANES
SLAB_ROWS = QUADS * (K + 1)
F8 = jnp.float8_e4m3fn
NT = (((1,), (1,)), ((), ()))
SKETCH_SCALES = (4.0, 64.0, 2.0**24, 2.0**29)
CURVE_SCALES = (1024.0, 2.0**14)
TERM_ROWS = LEAVES * K
W_ROWS = 288
OWN_BINS = 32
CHUNK = 4 * SLAB
PART = (LEAVES * (K + 1), OWN_BINS * FEATS)
ORDER = tuple((k, own) for k in (3, 2, 1, 0) for own in (False, True))
OTHER_COST = 1000
OWN_COST = 1000
ADD_COST = 1000
GROUP = 4
SKETCH_VMEM = 57 << 20


def sketch_kernel(scores_ref, targets_ref, signs_ref, out_ref, score_buf, target_buf, sems):
    x = lax.axis_index("x").astype(jnp.int32)

    def loads(slab):
        row = pl.multiple_of(((x ^ (slab // 4)) * 4 + slab % 4) * SLAB, SLAB)
        return (
            pltpu.make_async_copy(scores_ref.at[pl.ds(row, SLAB), :], score_buf.at[slab], sems.at[0, slab]),
            pltpu.make_async_copy(targets_ref.at[pl.ds(row, SLAB), :], target_buf.at[slab], sems.at[1, slab]),
        )

    for slab in range(16):
        for copy in loads(slab):
            copy.start()
    sign_matrix = (2 * signs_ref[...] - 1).astype(jnp.bfloat16)
    left = jnp.concatenate(
        [
            jnp.concatenate([sign_matrix, sign_matrix, jnp.zeros((K, LABS), jnp.bfloat16)], axis=1),
            jnp.concatenate(
                [jnp.zeros((K, 2 * LABS), jnp.bfloat16), jnp.ones((K, LABS), jnp.bfloat16)], axis=1
            ),
        ],
        axis=0,
    )
    for first in range(0, 16, GROUP):
        for slab in range(first, first + GROUP):
            for copy in loads(slab):
                copy.wait()
        scores = score_buf[first : first + GROUP].reshape(GROUP * SLAB, LABS).astype(jnp.float32)
        targets = target_buf[first : first + GROUP].reshape(GROUP * SLAB, LABS).astype(jnp.float32)
        half_tanh = 0.5 * jnp.tanh(0.5 * scores)
        gradient = half_tanh + (0.5 - targets)
        hessian = 0.25 - half_tanh * half_tanh
        hessian = hessian[:, :LANES] + hessian[:, LANES:]
        grad_high = gradient.astype(jnp.bfloat16)
        grad_low = (gradient - grad_high.astype(jnp.float32)).astype(jnp.bfloat16)
        hess_high = hessian.astype(jnp.bfloat16)
        hess_low = (hessian - hess_high.astype(jnp.float32)).astype(jnp.bfloat16)
        right = jnp.concatenate([grad_high, grad_low, hess_high, hess_low], axis=1)
        stats = lax.dot_general(left, right, NT, preferred_element_type=jnp.float32)
        for piece in range(GROUP * QUADS):
            slab, quad = first + piece // QUADS, piece % QUADS
            lanes = slice(piece * LANES, (piece + 1) * LANES)
            out_ref[slab // 4, slab % 4, quad * K : (quad + 1) * K, :] = stats[:K, lanes] * (
                1.0 / math.sqrt(L)
            )
            out_ref[slab // 4, slab % 4, QUADS * K + quad : QUADS * K + quad + 1, :] = stats[
                K : K + 1, lanes
            ] * (1.0 / L)


def sketch_call(scores, targets, signs_t):
    return pl.pallas_call(
        sketch_kernel,
        in_specs=[
            pl.BlockSpec(memory_space=pl.ANY),
            pl.BlockSpec(memory_space=pl.ANY),
            pl.BlockSpec(memory_space=pltpu.VMEM),
        ],
        out_specs=pl.BlockSpec(memory_space=pltpu.VMEM),
        out_shape=jax.ShapeDtypeStruct((4, 4, SLAB_ROWS, LANES), jnp.float32),
        scratch_shapes=[
            pltpu.VMEM((16, SLAB, LABS), jnp.bfloat16),
            pltpu.VMEM((16, SLAB, LABS), jnp.int32),
            pltpu.SemaphoreType.DMA((2, 16)),
        ],
        compiler_params=pltpu.CompilerParams(vmem_limit_bytes=SKETCH_VMEM),
        cost_estimate=pl.CostEstimate(
            flops=2 * ROWS * 768 * 32, bytes_accessed=ROWS * LABS * 6, transcendentals=ROWS * LABS
        ),
        name="sketch",
    )(scores, targets, signs_t)


def split_terms(values, scales):
    terms = []
    for scale in scales:
        term = (values * scale).astype(F8).astype(jnp.float32)
        terms.append(term)
        values = values - term * (1.0 / scale)
    return terms


def weight_block(stats_ref, leaves_ref, chunk, write):
    leaf_iota = lax.broadcasted_iota(jnp.int32, (8, LANES), 0)
    zeros = jnp.zeros((K, LANES), jnp.float32)
    for piece in range(4 * QUADS):
        slab, quad = piece // QUADS, piece % QUADS
        leaf = leaves_ref[pl.ds(chunk * 4 * QUADS + piece, 1), :]
        sketch = stats_ref[slab, quad * K : (quad + 1) * K, :]
        curve = stats_ref[slab, QUADS * K + quad : QUADS * K + quad + 1, :]
        sketch = sketch.astype(jnp.bfloat16).astype(jnp.float32)
        curve = jnp.broadcast_to(curve, (8, LANES)).astype(jnp.bfloat16).astype(jnp.float32)
        masks = [jnp.broadcast_to(leaf == e, (K, LANES)) for e in range(LEAVES)]
        curve_mask = jnp.broadcast_to(leaf, (8, LANES)) == leaf_iota
        parts = [
            jnp.where(mask, term, zeros) for term in split_terms(sketch, SKETCH_SCALES) for mask in masks
        ]
        parts += [jnp.where(curve_mask, term, 0.0) for term in split_terms(curve, CURVE_SCALES)]
        parts.append(jnp.zeros((W_ROWS - 4 * TERM_ROWS - 16, LANES), jnp.float32))
        write(piece, jnp.concatenate(parts, axis=0).astype(F8))


def weight_kernel(s1, s2, s3, leaves_ref, out_ref):
    x = lax.axis_index("x").astype(jnp.int32)
    for k, stats_ref in ((1, s1), (2, s2), (3, s3)):

        def write(piece, value, first=(k - 1) * CHUNK):
            out_ref[:, first + piece * LANES : first + (piece + 1) * LANES] = value

        weight_block(stats_ref, leaves_ref, x ^ k, write)


def weight_call(blocks, leaves):
    return pl.pallas_call(
        weight_kernel,
        in_specs=[pl.BlockSpec(memory_space=pltpu.VMEM)] * 4,
        out_specs=pl.BlockSpec(memory_space=pltpu.VMEM),
        out_shape=jax.ShapeDtypeStruct((W_ROWS, 3 * CHUNK), F8),
        compiler_params=pltpu.CompilerParams(vmem_limit_bytes=24 << 20),
        cost_estimate=pl.CostEstimate(flops=1_000_000, bytes_accessed=100_000, transcendentals=0),
        name="weights",
    )(*blocks, leaves)


def count(codes, weights):
    codes = jnp.clip(codes, -1, OWN_BINS)
    pair = jnp.concatenate([codes, codes - 1], axis=0).astype(jnp.int8)
    one = jnp.ones(pair.shape, F8)
    zero = jnp.zeros(pair.shape, F8)
    onehot = jnp.concatenate(
        [jnp.where(pair == jnp.int8(b), one, zero) for b in range(0, OWN_BINS, 2)], axis=0
    )
    total = lax.dot_general(weights, onehot, NT, preferred_element_type=jnp.float32)
    sketch = sum(
        total[t * TERM_ROWS : (t + 1) * TERM_ROWS] * (1.0 / scale) for t, scale in enumerate(SKETCH_SCALES)
    )
    curve = sum(
        total[4 * TERM_ROWS + 8 * t : 4 * TERM_ROWS + 8 * t + 8] * (1.0 / scale)
        for t, scale in enumerate(CURVE_SCALES)
    )
    return jnp.concatenate([sketch, curve[:LEAVES]], axis=0)


def first_bin(k, own):
    zl = lax.axis_index("zl").astype(jnp.int32)
    core = lax.axis_index("c").astype(jnp.int32)
    return OWN_BINS * (2 * (zl ^ k) + (core if own else 1 - core))


def own_kernel(bins_ref, stats_ref, leaves_ref, out_ref, weights_ref):
    x = lax.axis_index("x").astype(jnp.int32)

    def write(piece, value):
        weights_ref[:, piece * LANES : (piece + 1) * LANES] = value

    weight_block(stats_ref, leaves_ref, x, write)
    bins = bins_ref[:, pl.ds(pl.multiple_of(x * CHUNK, CHUNK), CHUNK)]
    for k, own in ORDER:
        out_ref[4 * own + k] = count(bins - first_bin(k, own), weights_ref[...])


def own_call(bins_t, stats, leaves):
    return pl.pallas_call(
        own_kernel,
        in_specs=[pl.BlockSpec(memory_space=pltpu.VMEM)] * 3,
        out_specs=pl.BlockSpec(memory_space=pltpu.VMEM),
        out_shape=jax.ShapeDtypeStruct((8,) + PART, jnp.float32),
        scratch_shapes=[pltpu.VMEM((W_ROWS, CHUNK), F8)],
        compiler_params=pltpu.CompilerParams(vmem_limit_bytes=32 << 20),
        cost_estimate=pl.CostEstimate(flops=5_000_000_000, bytes_accessed=1_000_000, transcendentals=0),
        name="own",
    )(bins_t, stats, leaves)


def rest_bins(bins_ref):
    x = lax.axis_index("x").astype(jnp.int32)
    return jnp.concatenate(
        [bins_ref[:, pl.ds(pl.multiple_of((x ^ j) * CHUNK, CHUNK), CHUNK)] for j in (1, 2, 3)], axis=1
    )


def other_kernel(ks, bins_ref, weights_ref, start_ref, out_ref):
    bins = rest_bins(bins_ref)
    for place, k in enumerate(ks):
        out_ref[place] = start_ref[k] + count(bins - first_bin(k, False), weights_ref[...])


def other_call(ks, bins_t, weights, start):
    return pl.pallas_call(
        functools.partial(other_kernel, ks),
        in_specs=[pl.BlockSpec(memory_space=pltpu.VMEM)] * 3,
        out_specs=pl.BlockSpec(memory_space=pltpu.VMEM),
        out_shape=jax.ShapeDtypeStruct((len(ks),) + PART, jnp.float32),
        compiler_params=pltpu.CompilerParams(vmem_limit_bytes=32 << 20),
        cost_estimate=pl.CostEstimate(flops=OTHER_COST * len(ks), bytes_accessed=1000, transcendentals=0),
        name="other",
    )(bins_t, weights, start)


def hist_kernel(k, place, bins_ref, weights_ref, start_ref, swapped_ref, *refs):
    out_ref = refs[-1]
    bins = rest_bins(bins_ref)
    total = start_ref[4 + k] + swapped_ref[place]
    for ref in refs[:-1]:
        total += ref[...]
    out_ref[...] = total + count(bins - first_bin(k, True), weights_ref[...])


def hist_call(k, bins_t, weights, start, swapped, place, *more):
    return pl.pallas_call(
        functools.partial(hist_kernel, k, place),
        in_specs=[pl.BlockSpec(memory_space=pltpu.VMEM)] * (4 + len(more)),
        out_specs=pl.BlockSpec(memory_space=pltpu.VMEM),
        out_shape=jax.ShapeDtypeStruct(PART, jnp.float32),
        compiler_params=pltpu.CompilerParams(vmem_limit_bytes=32 << 20),
        cost_estimate=pl.CostEstimate(flops=OWN_COST, bytes_accessed=1000, transcendentals=0),
        name="hist",
    )(bins_t, weights, start, swapped, *more)


def add_kernel(a_ref, b_ref, out_ref):
    out_ref[...] = a_ref[...] + b_ref[...]


def add_call(a, b):
    return pl.pallas_call(
        add_kernel,
        in_specs=[pl.BlockSpec(memory_space=pltpu.VMEM)] * 2,
        out_specs=pl.BlockSpec(memory_space=pltpu.VMEM),
        out_shape=jax.ShapeDtypeStruct(PART, jnp.float32),
        compiler_params=pltpu.CompilerParams(vmem_limit_bytes=8 << 20),
        cost_estimate=pl.CostEstimate(flops=ADD_COST, bytes_accessed=1000, transcendentals=0),
        name="add",
    )(a, b)


def finish_kernel(a_ref, b_ref, c_ref, out_ref):
    total = a_ref[...] + (b_ref[...] + c_ref[...])
    rows = []
    for e in range(LEAVES):
        rows.append(total[e * K : (e + 1) * K])
        rows.append(total[TERM_ROWS + e : TERM_ROWS + e + 1])
    total = jnp.concatenate(rows, axis=0)
    out_ref[...] = total.T.reshape(OWN_BINS, FEATS, LEAVES * (K + 1))


def finish_call(parts):
    return pl.pallas_call(
        finish_kernel,
        out_shape=jax.ShapeDtypeStruct((OWN_BINS, FEATS, LEAVES * (K + 1)), jnp.float32),
        compiler_params=pltpu.CompilerParams(vmem_limit_bytes=8 << 20),
        name="finish",
    )(*parts)


def swap(value, axis, bit, size):
    return lax.ppermute(value, axis, [(i, i ^ bit) for i in range(size)])


def per_device(scores, targets, signs, bins, leaves):
    signs_t = signs.T
    bins_t = bins.T
    leaves2 = leaves.reshape(ROWS // LANES, LANES)

    parts = sketch_call(scores, targets, signs_t)
    arrived = [swap(parts[k], "x", k, 4) for k in (2, 1, 3)]
    mine = (parts[0] + arrived[0]) + (arrived[1] + arrived[2])
    arrived = [swap(mine, "y", k, 4) for k in (2, 1, 3)]
    mine = (mine + arrived[0]) + (arrived[1] + arrived[2])
    mine = mine + swap(mine, "zh", 1, 2)
    blocks = [swap(mine, "x", k, 4) for k in (1, 2, 3)]
    start = own_call(bins_t, mine, leaves2)
    weights = weight_call(blocks, leaves2)

    first = swap(other_call((3,), bins_t, weights, start), "c", 1, 2)
    part = hist_call(3, bins_t, weights, start, first, 0)
    moved3 = swap(part, "zl", 3, 4)
    rest = swap(other_call((2, 1, 0), bins_t, weights, start), "c", 1, 2)
    part = hist_call(2, bins_t, weights, start, rest, 0)
    moved2 = swap(part, "zl", 2, 4)
    part = hist_call(1, bins_t, weights, start, rest, 1)
    moved1 = swap(part, "zl", 1, 4)
    part = hist_call(0, bins_t, weights, start, rest, 2, moved3)
    return finish_call((part, moved2, moved1))


def solution(mesh):
    fine = Mesh(mesh.devices.reshape(4, 2, 4, 4, 2), ("zl", "c", "y", "x", "zh"))
    row, lab = ("zl", "c"), ("y", "x", "zh")
    in_specs = (P(row, lab), P(row, lab), P(lab, None), P(row, lab), P(row))
    out_specs = P(row, lab, None)
    return jax.shard_map(
        per_device, mesh=fine, in_specs=in_specs, out_specs=out_specs, check_vma=False
    )
```

```python
import functools
import math

import jax
import jax.numpy as jnp
from jax import lax
from jax.experimental import pallas as pl
from jax.experimental.pallas import tpu as pltpu
from jax.sharding import Mesh, PartitionSpec as P

L = 8192
BINS = 256
K = 16
LEAVES = 4
ROWS = 8192
LABS = 256
FEATS = 16
SLAB = 512
LANES = 128
QUADS = SLAB // LANES
SLAB_ROWS = QUADS * (K + 1)
F8 = jnp.float8_e4m3fn
NT = (((1,), (1,)), ((), ()))
SKETCH_SCALES = (4.0, 64.0, 2.0**24, 2.0**29)
CURVE_SCALES = (1024.0, 2.0**14)
TERM_ROWS = LEAVES * K
W_ROWS = 288
OWN_BINS = 32
CHUNK = 4 * SLAB
PART = (LEAVES * (K + 1), OWN_BINS * FEATS)
ORDER = tuple((k, own) for k in (3, 2, 1, 0) for own in (False, True))
OTHER_COST = 1000
OWN_COST = 1000
LAST = 2
GROUP = 4
SKETCH_VMEM = 51 << 20


def sketch_kernel(ks, scores_ref, targets_ref, signs_ref, *refs):
    out_refs, (score_buf, target_buf, sems) = refs[: len(ks)], refs[len(ks) :]
    x = lax.axis_index("x").astype(jnp.int32)

    def loads(slab):
        row = pl.multiple_of(((x ^ ks[slab // 4]) * 4 + slab % 4) * SLAB, SLAB)
        return (
            pltpu.make_async_copy(scores_ref.at[pl.ds(row, SLAB), :], score_buf.at[slab], sems.at[0, slab]),
            pltpu.make_async_copy(targets_ref.at[pl.ds(row, SLAB), :], target_buf.at[slab], sems.at[1, slab]),
        )

    for slab in range(4 * len(ks)):
        for copy in loads(slab):
            copy.start()
    sign_matrix = (2 * signs_ref[...] - 1).astype(jnp.bfloat16)
    left = jnp.concatenate(
        [
            jnp.concatenate([sign_matrix, sign_matrix, jnp.zeros((K, LABS), jnp.bfloat16)], axis=1),
            jnp.concatenate(
                [jnp.zeros((K, 2 * LABS), jnp.bfloat16), jnp.ones((K, LABS), jnp.bfloat16)], axis=1
            ),
        ],
        axis=0,
    )
    for first in range(0, 4 * len(ks), GROUP):
        for slab in range(first, first + GROUP):
            for copy in loads(slab):
                copy.wait()
        scores = score_buf[first : first + GROUP].reshape(GROUP * SLAB, LABS).astype(jnp.float32)
        targets = target_buf[first : first + GROUP].reshape(GROUP * SLAB, LABS).astype(jnp.float32)
        half_tanh = 0.5 * jnp.tanh(0.5 * scores)
        gradient = half_tanh + (0.5 - targets)
        hessian = 0.25 - half_tanh * half_tanh
        hessian = hessian[:, :LANES] + hessian[:, LANES:]
        grad_high = gradient.astype(jnp.bfloat16)
        grad_low = (gradient - grad_high.astype(jnp.float32)).astype(jnp.bfloat16)
        hess_high = hessian.astype(jnp.bfloat16)
        hess_low = (hessian - hess_high.astype(jnp.float32)).astype(jnp.bfloat16)
        right = jnp.concatenate([grad_high, grad_low, hess_high, hess_low], axis=1)
        stats = lax.dot_general(left, right, NT, preferred_element_type=jnp.float32)
        for piece in range(GROUP * QUADS):
            slab, quad = first + piece // QUADS, piece % QUADS
            lanes = slice(piece * LANES, (piece + 1) * LANES)
            out_ref, at = out_refs[slab // 4], slab % 4
            out_ref[at, quad * K : (quad + 1) * K, :] = stats[:K, lanes] * (1.0 / math.sqrt(L))
            out_ref[at, QUADS * K + quad : QUADS * K + quad + 1, :] = stats[K : K + 1, lanes] * (1.0 / L)


def sketch_call(ks, scores, targets, signs_t):
    slabs = 4 * len(ks)
    return pl.pallas_call(
        functools.partial(sketch_kernel, ks),
        in_specs=[
            pl.BlockSpec(memory_space=pl.ANY),
            pl.BlockSpec(memory_space=pl.ANY),
            pl.BlockSpec(memory_space=pltpu.VMEM),
        ],
        out_specs=[pl.BlockSpec(memory_space=pltpu.VMEM)] * len(ks),
        out_shape=[jax.ShapeDtypeStruct((4, SLAB_ROWS, LANES), jnp.float32)] * len(ks),
        scratch_shapes=[
            pltpu.VMEM((slabs, SLAB, LABS), jnp.bfloat16),
            pltpu.VMEM((slabs, SLAB, LABS), jnp.int32),
            pltpu.SemaphoreType.DMA((2, slabs)),
        ],
        compiler_params=pltpu.CompilerParams(vmem_limit_bytes=SKETCH_VMEM),
        cost_estimate=pl.CostEstimate(
            flops=2 * slabs * SLAB * 768 * 32,
            bytes_accessed=slabs * SLAB * LABS * 6,
            transcendentals=slabs * SLAB * LABS,
        ),
        name="sketch",
    )(scores, targets, signs_t)


def split_terms(values, scales):
    terms = []
    for scale in scales:
        term = (values * scale).astype(F8).astype(jnp.float32)
        terms.append(term)
        values = values - term * (1.0 / scale)
    return terms


def weight_block(stats_ref, leaves_ref, chunk, write):
    leaf_iota = lax.broadcasted_iota(jnp.int32, (8, LANES), 0)
    zeros = jnp.zeros((K, LANES), jnp.float32)
    for piece in range(4 * QUADS):
        slab, quad = piece // QUADS, piece % QUADS
        leaf = leaves_ref[pl.ds(chunk * 4 * QUADS + piece, 1), :]
        sketch = stats_ref[slab, quad * K : (quad + 1) * K, :]
        curve = stats_ref[slab, QUADS * K + quad : QUADS * K + quad + 1, :]
        sketch = sketch.astype(jnp.bfloat16).astype(jnp.float32)
        curve = jnp.broadcast_to(curve, (8, LANES)).astype(jnp.bfloat16).astype(jnp.float32)
        masks = [jnp.broadcast_to(leaf == e, (K, LANES)) for e in range(LEAVES)]
        curve_mask = jnp.broadcast_to(leaf, (8, LANES)) == leaf_iota
        parts = [
            jnp.where(mask, term, zeros) for term in split_terms(sketch, SKETCH_SCALES) for mask in masks
        ]
        parts += [jnp.where(curve_mask, term, 0.0) for term in split_terms(curve, CURVE_SCALES)]
        parts.append(jnp.zeros((W_ROWS - 4 * TERM_ROWS - 16, LANES), jnp.float32))
        write(piece, jnp.concatenate(parts, axis=0).astype(F8))


def weight_kernel(k, stats_ref, leaves_ref, out_ref):
    x = lax.axis_index("x").astype(jnp.int32)

    def write(piece, value):
        out_ref[:, piece * LANES : (piece + 1) * LANES] = value

    weight_block(stats_ref, leaves_ref, x ^ k, write)


def weight_call(k, stats, leaves):
    return pl.pallas_call(
        functools.partial(weight_kernel, k),
        in_specs=[pl.BlockSpec(memory_space=pltpu.VMEM)] * 2,
        out_specs=pl.BlockSpec(memory_space=pltpu.VMEM),
        out_shape=jax.ShapeDtypeStruct((W_ROWS, CHUNK), F8),
        compiler_params=pltpu.CompilerParams(vmem_limit_bytes=24 << 20),
        cost_estimate=pl.CostEstimate(flops=1_000_000, bytes_accessed=100_000, transcendentals=0),
        name="weights",
    )(stats, leaves)


def count(codes, weights):
    codes = jnp.clip(codes, -1, OWN_BINS)
    pair = jnp.concatenate([codes, codes - 1], axis=0).astype(jnp.int8)
    one = jnp.ones(pair.shape, F8)
    zero = jnp.zeros(pair.shape, F8)
    onehot = jnp.concatenate(
        [jnp.where(pair == jnp.int8(b), one, zero) for b in range(0, OWN_BINS, 2)], axis=0
    )
    total = lax.dot_general(weights, onehot, NT, preferred_element_type=jnp.float32)
    sketch = sum(
        total[t * TERM_ROWS : (t + 1) * TERM_ROWS] * (1.0 / scale) for t, scale in enumerate(SKETCH_SCALES)
    )
    curve = sum(
        total[4 * TERM_ROWS + 8 * t : 4 * TERM_ROWS + 8 * t + 8] * (1.0 / scale)
        for t, scale in enumerate(CURVE_SCALES)
    )
    return jnp.concatenate([sketch, curve[:LEAVES]], axis=0)


def first_bin(k, own):
    zl = lax.axis_index("zl").astype(jnp.int32)
    core = lax.axis_index("c").astype(jnp.int32)
    return OWN_BINS * (2 * (zl ^ k) + (core if own else 1 - core))


def block_bins(bins_ref, k):
    x = lax.axis_index("x").astype(jnp.int32)
    return bins_ref[:, pl.ds(pl.multiple_of((x ^ k) * CHUNK, CHUNK), CHUNK)]


def block_kernel(k, bins_ref, stats_ref, leaves_ref, *refs):
    out_ref, weights_ref = refs[-2:]
    weight_kernel(k, stats_ref, leaves_ref, weights_ref)
    bins = block_bins(bins_ref, k)
    for to, own in ORDER:
        total = count(bins - first_bin(to, own), weights_ref[...])
        if len(refs) == 3:
            total += refs[0][4 * own + to]
        out_ref[4 * own + to] = total


def block_call(k, bins_t, stats, leaves, *before):
    return pl.pallas_call(
        functools.partial(block_kernel, k),
        in_specs=[pl.BlockSpec(memory_space=pltpu.VMEM)] * (3 + len(before)),
        out_specs=pl.BlockSpec(memory_space=pltpu.VMEM),
        out_shape=jax.ShapeDtypeStruct((8,) + PART, jnp.float32),
        scratch_shapes=[pltpu.VMEM((W_ROWS, CHUNK), F8)],
        compiler_params=pltpu.CompilerParams(vmem_limit_bytes=32 << 20),
        cost_estimate=pl.CostEstimate(flops=5_000_000_000, bytes_accessed=1_000_000, transcendentals=0),
        name="block",
    )(bins_t, stats, leaves, *before)


def other_kernel(ks, bins_ref, weights_ref, start_ref, out_ref):
    bins = block_bins(bins_ref, LAST)
    for place, k in enumerate(ks):
        out_ref[place] = start_ref[k] + count(bins - first_bin(k, False), weights_ref[...])


def other_call(ks, bins_t, weights, start):
    return pl.pallas_call(
        functools.partial(other_kernel, ks),
        in_specs=[pl.BlockSpec(memory_space=pltpu.VMEM)] * 3,
        out_specs=pl.BlockSpec(memory_space=pltpu.VMEM),
        out_shape=jax.ShapeDtypeStruct((len(ks),) + PART, jnp.float32),
        compiler_params=pltpu.CompilerParams(vmem_limit_bytes=32 << 20),
        cost_estimate=pl.CostEstimate(flops=OTHER_COST * len(ks), bytes_accessed=1000, transcendentals=0),
        name="other",
    )(bins_t, weights, start)


def hist_kernel(k, place, bins_ref, weights_ref, start_ref, swapped_ref, *refs):
    out_ref = refs[-1]
    bins = block_bins(bins_ref, LAST)
    total = start_ref[4 + k] + swapped_ref[place]
    for ref in refs[:-1]:
        total += ref[...]
    out_ref[...] = total + count(bins - first_bin(k, True), weights_ref[...])


def hist_call(k, bins_t, weights, start, swapped, place, *more):
    return pl.pallas_call(
        functools.partial(hist_kernel, k, place),
        in_specs=[pl.BlockSpec(memory_space=pltpu.VMEM)] * (4 + len(more)),
        out_specs=pl.BlockSpec(memory_space=pltpu.VMEM),
        out_shape=jax.ShapeDtypeStruct(PART, jnp.float32),
        compiler_params=pltpu.CompilerParams(vmem_limit_bytes=32 << 20),
        cost_estimate=pl.CostEstimate(flops=OWN_COST, bytes_accessed=1000, transcendentals=0),
        name="hist",
    )(bins_t, weights, start, swapped, *more)


def finish_kernel(a_ref, b_ref, c_ref, out_ref):
    total = a_ref[...] + (b_ref[...] + c_ref[...])
    rows = []
    for e in range(LEAVES):
        rows.append(total[e * K : (e + 1) * K])
        rows.append(total[TERM_ROWS + e : TERM_ROWS + e + 1])
    total = jnp.concatenate(rows, axis=0)
    out_ref[...] = total.T.reshape(OWN_BINS, FEATS, LEAVES * (K + 1))


def finish_call(parts):
    return pl.pallas_call(
        finish_kernel,
        out_shape=jax.ShapeDtypeStruct((OWN_BINS, FEATS, LEAVES * (K + 1)), jnp.float32),
        compiler_params=pltpu.CompilerParams(vmem_limit_bytes=8 << 20),
        name="finish",
    )(*parts)


def swap(value, axis, bit, size):
    return lax.ppermute(value, axis, [(i, i ^ bit) for i in range(size)])


def per_device(scores, targets, signs, bins, leaves):
    signs_t = signs.T
    bins_t = bins.T
    leaves2 = leaves.reshape(ROWS // LANES, LANES)

    arrived = [
        swap(part, "x", k, 4) for k, part in zip((2, 1, 3), sketch_call((2, 1, 3), scores, targets, signs_t))
    ]
    (mine,) = sketch_call((0,), scores, targets, signs_t)
    mine = (mine + arrived[0]) + (arrived[1] + arrived[2])
    arrived = [swap(mine, "y", k, 4) for k in (2, 1, 3)]
    mine = (mine + arrived[0]) + (arrived[1] + arrived[2])
    mine = mine + swap(mine, "zh", 1, 2)
    blocks = {k: swap(mine, "x", k, 4) for k in (1, 3, 2)}
    start = block_call(0, bins_t, mine, leaves2)
    for k in (1, 3):
        start = block_call(k, bins_t, blocks[k], leaves2, start)
    weights = weight_call(LAST, blocks[LAST], leaves2)

    far = swap(other_call((3, 2), bins_t, weights, start), "c", 1, 2)
    near = swap(other_call((1, 0), bins_t, weights, start), "c", 1, 2)
    passed = swap(hist_call(3, bins_t, weights, start, far, 0), "zl", 1, 4)
    moved1 = swap(hist_call(1, bins_t, weights, start, near, 0), "zl", 1, 4)
    moved2 = swap(hist_call(2, bins_t, weights, start, far, 1, passed), "zl", 2, 4)
    part = hist_call(0, bins_t, weights, start, near, 1)
    return finish_call((part, moved2, moved1))


def solution(mesh):
    fine = Mesh(mesh.devices.reshape(4, 2, 4, 4, 2), ("zl", "c", "y", "x", "zh"))
    row, lab = ("zl", "c"), ("y", "x", "zh")
    in_specs = (P(row, lab), P(row, lab), P(lab, None), P(row, lab), P(row))
    out_specs = P(row, lab, None)
    return jax.shard_map(
        per_device, mesh=fine, in_specs=in_specs, out_specs=out_specs, check_vma=False
    )
```

```python
import functools
import math

import jax
import jax.numpy as jnp
from jax import lax
from jax.experimental import pallas as pl
from jax.experimental.pallas import tpu as pltpu
from jax.sharding import Mesh, PartitionSpec as P

L = 8192
BINS = 256
K = 16
LEAVES = 4
ROWS = 8192
LABS = 256
FEATS = 16
SLAB = 512
LANES = 128
QUADS = SLAB // LANES
PIECES = 4 * QUADS
STAT_ROWS = PIECES * (K + 1)
F8 = jnp.float8_e4m3fn
NT = (((1,), (1,)), ((), ()))
SKETCH_SCALES = (4.0, 64.0, 2.0**24, 2.0**29)
CURVE_SCALES = (1024.0, 2.0**14)
TERM_ROWS = LEAVES * K
W_ROWS = 288
OWN_BINS = 32
CHUNK = 4 * SLAB
HALF = OWN_BINS * FEATS // 2
PART = (2 * LEAVES * (K + 1), HALF)
ORDER = tuple((k, own) for k in (3, 2, 1, 0) for own in (False, True))
OTHER_COST = 1000
HIST_COST = (1000, 1000, 5_000_000_000, 1000)
LAST = (3, 2)
GROUP = 4
SKETCH_VMEM = 51 << 20


def sketch_kernel(ks, scores_ref, targets_ref, signs_ref, *refs):
    out_refs, (score_buf, target_buf, sems) = refs[: len(ks)], refs[len(ks) :]
    x = lax.axis_index("x").astype(jnp.int32)

    def loads(slab):
        row = pl.multiple_of(((x ^ ks[slab // 4]) * 4 + slab % 4) * SLAB, SLAB)
        return (
            pltpu.make_async_copy(scores_ref.at[pl.ds(row, SLAB), :], score_buf.at[slab], sems.at[0, slab]),
            pltpu.make_async_copy(targets_ref.at[pl.ds(row, SLAB), :], target_buf.at[slab], sems.at[1, slab]),
        )

    for slab in range(4 * len(ks)):
        for copy in loads(slab):
            copy.start()
    sign_matrix = (2 * signs_ref[...] - 1).astype(jnp.bfloat16)
    left = jnp.concatenate(
        [
            jnp.concatenate([sign_matrix, sign_matrix, jnp.zeros((K, LABS), jnp.bfloat16)], axis=1),
            jnp.concatenate(
                [jnp.zeros((K, 2 * LABS), jnp.bfloat16), jnp.ones((K, LABS), jnp.bfloat16)], axis=1
            ),
        ],
        axis=0,
    )
    for first in range(0, 4 * len(ks), GROUP):
        for slab in range(first, first + GROUP):
            for copy in loads(slab):
                copy.wait()
        scores = score_buf[first : first + GROUP].reshape(GROUP * SLAB, LABS).astype(jnp.float32)
        targets = target_buf[first : first + GROUP].reshape(GROUP * SLAB, LABS).astype(jnp.float32)
        half_tanh = 0.5 * jnp.tanh(0.5 * scores)
        gradient = half_tanh + (0.5 - targets)
        hessian = 0.25 - half_tanh * half_tanh
        hessian = hessian[:, :LANES] + hessian[:, LANES:]
        grad_high = gradient.astype(jnp.bfloat16)
        grad_low = (gradient - grad_high.astype(jnp.float32)).astype(jnp.bfloat16)
        hess_high = hessian.astype(jnp.bfloat16)
        hess_low = (hessian - hess_high.astype(jnp.float32)).astype(jnp.bfloat16)
        right = jnp.concatenate([grad_high, grad_low, hess_high, hess_low], axis=1)
        stats = lax.dot_general(left, right, NT, preferred_element_type=jnp.float32)
        for piece in range(GROUP * QUADS):
            at, lanes = piece % PIECES, slice(piece * LANES, (piece + 1) * LANES)
            out_ref = out_refs[(first * QUADS + piece) // PIECES]
            out_ref[at * K : (at + 1) * K, :] = stats[:K, lanes] * (1.0 / math.sqrt(L))
            out_ref[PIECES * K + at : PIECES * K + at + 1, :] = stats[K : K + 1, lanes] * (1.0 / L)


def sketch_call(ks, scores, targets, signs_t):
    slabs = 4 * len(ks)
    return pl.pallas_call(
        functools.partial(sketch_kernel, ks),
        in_specs=[
            pl.BlockSpec(memory_space=pl.ANY),
            pl.BlockSpec(memory_space=pl.ANY),
            pl.BlockSpec(memory_space=pltpu.VMEM),
        ],
        out_specs=[pl.BlockSpec(memory_space=pltpu.VMEM)] * len(ks),
        out_shape=[jax.ShapeDtypeStruct((STAT_ROWS, LANES), jnp.float32)] * len(ks),
        scratch_shapes=[
            pltpu.VMEM((slabs, SLAB, LABS), jnp.bfloat16),
            pltpu.VMEM((slabs, SLAB, LABS), jnp.int32),
            pltpu.SemaphoreType.DMA((2, slabs)),
        ],
        compiler_params=pltpu.CompilerParams(vmem_limit_bytes=SKETCH_VMEM),
        cost_estimate=pl.CostEstimate(
            flops=2 * slabs * SLAB * 768 * 32,
            bytes_accessed=slabs * SLAB * LABS * 6,
            transcendentals=slabs * SLAB * LABS,
        ),
        name="sketch",
    )(scores, targets, signs_t)


def split_terms(values, scales):
    terms = []
    for scale in scales:
        term = (values * scale).astype(F8).astype(jnp.float32)
        terms.append(term)
        values = values - term * (1.0 / scale)
    return terms


def weight_block(stats_ref, leaves_ref, chunk, write):
    leaf_iota = lax.broadcasted_iota(jnp.int32, (8, LANES), 0)
    zeros = jnp.zeros((K, LANES), jnp.float32)
    for piece in range(PIECES):
        leaf = leaves_ref[pl.ds(chunk * PIECES + piece, 1), :]
        sketch = stats_ref[piece * K : (piece + 1) * K, :]
        curve = stats_ref[PIECES * K + piece : PIECES * K + piece + 1, :]
        sketch = sketch.astype(jnp.bfloat16).astype(jnp.float32)
        curve = jnp.broadcast_to(curve, (8, LANES)).astype(jnp.bfloat16).astype(jnp.float32)
        masks = [jnp.broadcast_to(leaf == e, (K, LANES)) for e in range(LEAVES)]
        curve_mask = jnp.broadcast_to(leaf, (8, LANES)) == leaf_iota
        parts = [
            jnp.where(mask, term, zeros) for term in split_terms(sketch, SKETCH_SCALES) for mask in masks
        ]
        parts += [jnp.where(curve_mask, term, 0.0) for term in split_terms(curve, CURVE_SCALES)]
        parts.append(jnp.zeros((W_ROWS - 4 * TERM_ROWS - 16, LANES), jnp.float32))
        write(piece, jnp.concatenate(parts, axis=0).astype(F8))


def weight_kernel(ks, *refs):
    x = lax.axis_index("x").astype(jnp.int32)
    leaves_ref, out_ref = refs[-2:]
    for place, k in enumerate(ks):

        def write(piece, value, first=place * CHUNK):
            out_ref[:, first + piece * LANES : first + (piece + 1) * LANES] = value

        weight_block(refs[place], leaves_ref, x ^ k, write)


def weight_call(ks, stats, leaves):
    return pl.pallas_call(
        functools.partial(weight_kernel, ks),
        in_specs=[pl.BlockSpec(memory_space=pltpu.VMEM)] * (len(ks) + 1),
        out_specs=pl.BlockSpec(memory_space=pltpu.VMEM),
        out_shape=jax.ShapeDtypeStruct((W_ROWS, len(ks) * CHUNK), F8),
        compiler_params=pltpu.CompilerParams(vmem_limit_bytes=24 << 20),
        cost_estimate=pl.CostEstimate(flops=1_000_000, bytes_accessed=100_000, transcendentals=0),
        name="weights",
    )(*stats, leaves)


def count(codes, weights):
    codes = jnp.clip(codes, -1, OWN_BINS)
    pair = jnp.concatenate([codes, codes - 1], axis=0).astype(jnp.int8)
    one = jnp.ones(pair.shape, F8)
    zero = jnp.zeros(pair.shape, F8)
    onehot = jnp.concatenate(
        [jnp.where(pair == jnp.int8(b), one, zero) for b in range(0, OWN_BINS, 2)], axis=0
    )
    total = lax.dot_general(weights, onehot, NT, preferred_element_type=jnp.float32)
    sketch = sum(
        total[t * TERM_ROWS : (t + 1) * TERM_ROWS] * (1.0 / scale) for t, scale in enumerate(SKETCH_SCALES)
    )
    curve = sum(
        total[4 * TERM_ROWS + 8 * t : 4 * TERM_ROWS + 8 * t + 8] * (1.0 / scale)
        for t, scale in enumerate(CURVE_SCALES)
    )
    return jnp.concatenate(
        [sketch[:, :HALF], sketch[:, HALF:], curve[:LEAVES, :HALF], curve[:LEAVES, HALF:]], axis=0
    )


def first_bin(k, own):
    zl = lax.axis_index("zl").astype(jnp.int32)
    core = lax.axis_index("c").astype(jnp.int32)
    return OWN_BINS * (2 * (zl ^ k) + (core if own else 1 - core))


def block_bins(bins_ref, ks):
    x = lax.axis_index("x").astype(jnp.int32)
    return jnp.concatenate(
        [bins_ref[:, pl.ds(pl.multiple_of((x ^ k) * CHUNK, CHUNK), CHUNK)] for k in ks], axis=1
    )


def block_kernel(k, bins_ref, stats_ref, leaves_ref, *refs):
    out_ref, weights_ref = refs[-2:]
    weight_kernel((k,), stats_ref, leaves_ref, weights_ref)
    bins = block_bins(bins_ref, (k,))
    for to, own in ORDER:
        total = count(bins - first_bin(to, own), weights_ref[...])
        if len(refs) == 3:
            total += refs[0][4 * own + to]
        out_ref[4 * own + to] = total


def block_call(k, bins_t, stats, leaves, *before):
    return pl.pallas_call(
        functools.partial(block_kernel, k),
        in_specs=[pl.BlockSpec(memory_space=pltpu.VMEM)] * (3 + len(before)),
        out_specs=pl.BlockSpec(memory_space=pltpu.VMEM),
        out_shape=jax.ShapeDtypeStruct((8,) + PART, jnp.float32),
        scratch_shapes=[pltpu.VMEM((W_ROWS, CHUNK), F8)],
        compiler_params=pltpu.CompilerParams(vmem_limit_bytes=32 << 20),
        cost_estimate=pl.CostEstimate(flops=5_000_000_000, bytes_accessed=1_000_000, transcendentals=0),
        name="block",
    )(bins_t, stats, leaves, *before)


def other_kernel(ks, bins_ref, weights_ref, start_ref, out_ref):
    bins = block_bins(bins_ref, LAST)
    for place, k in enumerate(ks):
        out_ref[place] = start_ref[k] + count(bins - first_bin(k, False), weights_ref[...])


def other_call(ks, bins_t, weights, start):
    return pl.pallas_call(
        functools.partial(other_kernel, ks),
        in_specs=[pl.BlockSpec(memory_space=pltpu.VMEM)] * 3,
        out_specs=pl.BlockSpec(memory_space=pltpu.VMEM),
        out_shape=jax.ShapeDtypeStruct((len(ks),) + PART, jnp.float32),
        compiler_params=pltpu.CompilerParams(vmem_limit_bytes=32 << 20),
        cost_estimate=pl.CostEstimate(flops=OTHER_COST * len(ks), bytes_accessed=1000, transcendentals=0),
        name="other",
    )(bins_t, weights, start)


def hist_kernel(k, place, bins_ref, weights_ref, start_ref, swapped_ref, *refs):
    out_ref = refs[-1]
    bins = block_bins(bins_ref, LAST)
    total = start_ref[4 + k] + swapped_ref[place]
    for ref in refs[:-1]:
        total += ref[...]
    out_ref[...] = total + count(bins - first_bin(k, True), weights_ref[...])


def hist_call(k, bins_t, weights, start, swapped, place, *more):
    return pl.pallas_call(
        functools.partial(hist_kernel, k, place),
        in_specs=[pl.BlockSpec(memory_space=pltpu.VMEM)] * (4 + len(more)),
        out_specs=pl.BlockSpec(memory_space=pltpu.VMEM),
        out_shape=jax.ShapeDtypeStruct(PART, jnp.float32),
        compiler_params=pltpu.CompilerParams(vmem_limit_bytes=32 << 20),
        cost_estimate=pl.CostEstimate(flops=HIST_COST[k], bytes_accessed=1000, transcendentals=0),
        name="hist",
    )(bins_t, weights, start, swapped, *more)


def finish_kernel(a_ref, b_ref, c_ref, out_ref):
    total = a_ref[...] + (b_ref[...] + c_ref[...])
    for half in range(2):
        rows = []
        for e in range(LEAVES):
            first = half * TERM_ROWS + e * K
            rows.append(total[first : first + K])
            first = 2 * TERM_ROWS + half * LEAVES + e
            rows.append(total[first : first + 1])
        part = jnp.concatenate(rows, axis=0).T
        bins = OWN_BINS // 2
        out_ref[half * bins : (half + 1) * bins] = part.reshape(bins, FEATS, LEAVES * (K + 1))


def finish_call(parts):
    return pl.pallas_call(
        finish_kernel,
        out_shape=jax.ShapeDtypeStruct((OWN_BINS, FEATS, LEAVES * (K + 1)), jnp.float32),
        compiler_params=pltpu.CompilerParams(vmem_limit_bytes=8 << 20),
        name="finish",
    )(*parts)


def swap(value, axis, bit, size):
    return lax.ppermute(value, axis, [(i, i ^ bit) for i in range(size)])


def per_device(scores, targets, signs, bins, leaves):
    signs_t = signs.T
    bins_t = bins.T
    leaves2 = leaves.reshape(ROWS // LANES, LANES)

    arrived = [
        swap(part, "x", k, 4) for k, part in zip((2, 1, 3), sketch_call((2, 1, 3), scores, targets, signs_t))
    ]
    (mine,) = sketch_call((0,), scores, targets, signs_t)
    mine = (mine + arrived[0]) + (arrived[1] + arrived[2])
    arrived = [swap(mine, "y", k, 4) for k in (2, 1, 3)]
    mine = (mine + arrived[0]) + (arrived[1] + arrived[2])
    mine = mine + swap(mine, "zh", 1, 2)
    first = swap(mine, "x", 1, 4)
    start = block_call(0, bins_t, mine, leaves2)
    mine, start = lax.optimization_barrier((mine, start))
    last = [swap(mine, "x", k, 4) for k in LAST]
    start = block_call(1, bins_t, first, leaves2, start)
    weights = weight_call(LAST, last, leaves2)

    far = swap(other_call((3,), bins_t, weights, start), "c", 1, 2)
    mid = other_call((2,), bins_t, weights, start)
    mid, start = lax.optimization_barrier((mid, start))
    mid = swap(mid, "c", 1, 2)
    part = hist_call(3, bins_t, weights, start, far, 0)
    part, start = lax.optimization_barrier((part, start))
    passed = swap(part, "zl", 1, 4)
    near = swap(other_call((1, 0), bins_t, weights, start), "c", 1, 2)
    moved1 = swap(hist_call(1, bins_t, weights, start, near, 0), "zl", 1, 4)
    moved2 = swap(hist_call(2, bins_t, weights, start, mid, 0, passed), "zl", 2, 4)
    part = hist_call(0, bins_t, weights, start, near, 1)
    return finish_call((part, moved2, moved1))


def solution(mesh):
    fine = Mesh(mesh.devices.reshape(4, 2, 4, 4, 2), ("zl", "c", "y", "x", "zh"))
    row, lab = ("zl", "c"), ("y", "x", "zh")
    in_specs = (P(row, lab), P(row, lab), P(lab, None), P(row, lab), P(row))
    out_specs = P(row, lab, None)
    return jax.shard_map(
        per_device, mesh=fine, in_specs=in_specs, out_specs=out_specs, check_vma=False
    )
```

```python
import functools
import math

import jax
import jax.numpy as jnp
from jax import lax
from jax.experimental import pallas as pl
from jax.experimental.pallas import tpu as pltpu
from jax.sharding import Mesh, PartitionSpec as P

L = 8192
BINS = 256
K = 16
LEAVES = 4
ROWS = 8192
LABS = 256
FEATS = 16
SLAB = 512
LANES = 128
QUADS = SLAB // LANES
PIECES = 4 * QUADS
STAT_ROWS = PIECES * (K + 1)
F8 = jnp.float8_e4m3fn
NT = (((1,), (1,)), ((), ()))
SKETCH_SCALES = (4.0, 64.0, 2.0**24, 2.0**29)
CURVE_SCALES = (1024.0, 2.0**14)
TERM_ROWS = LEAVES * K
W_ROWS = 288
OWN_BINS = 32
CHUNK = 4 * SLAB
HALF = OWN_BINS * FEATS // 2
PART = (2 * LEAVES * (K + 1), HALF)
ORDER = tuple((k, own) for k in (3, 2, 1, 0) for own in (False, True))
OTHER_COST = 2_000_000_000
HIST_COST = (1000, 1000, 5_000_000_000, 1000)
LAST = (3, 2)
GROUP = 4
SKETCH_VMEM = 51 << 20


def sketch_kernel(ks, scores_ref, targets_ref, signs_ref, *refs):
    more_refs, out_refs = refs[: -3 - len(ks)], refs[-3 - len(ks) : -3]
    score_buf, target_buf, sems = refs[-3:]
    x = lax.axis_index("x").astype(jnp.int32)

    def loads(slab):
        row = pl.multiple_of(((x ^ ks[slab // 4]) * 4 + slab % 4) * SLAB, SLAB)
        return (
            pltpu.make_async_copy(scores_ref.at[pl.ds(row, SLAB), :], score_buf.at[slab], sems.at[0, slab]),
            pltpu.make_async_copy(targets_ref.at[pl.ds(row, SLAB), :], target_buf.at[slab], sems.at[1, slab]),
        )

    for slab in range(4 * len(ks)):
        for copy in loads(slab):
            copy.start()
    sign_matrix = (2 * signs_ref[...] - 1).astype(jnp.bfloat16)
    left = jnp.concatenate(
        [
            jnp.concatenate([sign_matrix, sign_matrix, jnp.zeros((K, LABS), jnp.bfloat16)], axis=1),
            jnp.concatenate(
                [jnp.zeros((K, 2 * LABS), jnp.bfloat16), jnp.ones((K, LABS), jnp.bfloat16)], axis=1
            ),
        ],
        axis=0,
    )
    for first in range(0, 4 * len(ks), GROUP):
        for slab in range(first, first + GROUP):
            for copy in loads(slab):
                copy.wait()
        scores = score_buf[first : first + GROUP].reshape(GROUP * SLAB, LABS).astype(jnp.float32)
        targets = target_buf[first : first + GROUP].reshape(GROUP * SLAB, LABS).astype(jnp.float32)
        half_tanh = 0.5 * jnp.tanh(0.5 * scores)
        gradient = half_tanh + (0.5 - targets)
        hessian = 0.25 - half_tanh * half_tanh
        hessian = hessian[:, :LANES] + hessian[:, LANES:]
        grad_high = gradient.astype(jnp.bfloat16)
        grad_low = (gradient - grad_high.astype(jnp.float32)).astype(jnp.bfloat16)
        hess_high = hessian.astype(jnp.bfloat16)
        hess_low = (hessian - hess_high.astype(jnp.float32)).astype(jnp.bfloat16)
        right = jnp.concatenate([grad_high, grad_low, hess_high, hess_low], axis=1)
        stats = lax.dot_general(left, right, NT, preferred_element_type=jnp.float32)
        for piece in range(GROUP * QUADS):
            at, lanes = piece % PIECES, slice(piece * LANES, (piece + 1) * LANES)
            out_ref = out_refs[(first * QUADS + piece) // PIECES]
            rows, row = slice(at * K, (at + 1) * K), slice(PIECES * K + at, PIECES * K + at + 1)
            sketch = stats[:K, lanes] * (1.0 / math.sqrt(L))
            curve = stats[K : K + 1, lanes] * (1.0 / L)
            for more_ref in more_refs:
                sketch += more_ref[rows, :]
                curve += more_ref[row, :]
            out_ref[rows, :] = sketch
            out_ref[row, :] = curve


def sketch_call(ks, scores, targets, signs_t, *more):
    slabs = 4 * len(ks)
    return pl.pallas_call(
        functools.partial(sketch_kernel, ks),
        in_specs=[
            pl.BlockSpec(memory_space=pl.ANY),
            pl.BlockSpec(memory_space=pl.ANY),
        ]
        + [pl.BlockSpec(memory_space=pltpu.VMEM)] * (1 + len(more)),
        out_specs=[pl.BlockSpec(memory_space=pltpu.VMEM)] * len(ks),
        out_shape=[jax.ShapeDtypeStruct((STAT_ROWS, LANES), jnp.float32)] * len(ks),
        scratch_shapes=[
            pltpu.VMEM((slabs, SLAB, LABS), jnp.bfloat16),
            pltpu.VMEM((slabs, SLAB, LABS), jnp.int32),
            pltpu.SemaphoreType.DMA((2, slabs)),
        ],
        compiler_params=pltpu.CompilerParams(vmem_limit_bytes=SKETCH_VMEM),
        cost_estimate=pl.CostEstimate(
            flops=2 * slabs * SLAB * 768 * 32,
            bytes_accessed=slabs * SLAB * LABS * 6,
            transcendentals=slabs * SLAB * LABS,
        ),
        name="sketch",
    )(scores, targets, signs_t, *more)


def split_terms(values, scales):
    terms = []
    for scale in scales:
        term = (values * scale).astype(F8).astype(jnp.float32)
        terms.append(term)
        values = values - term * (1.0 / scale)
    return terms


def weight_block(stats_ref, leaves_ref, chunk, write):
    leaf_iota = lax.broadcasted_iota(jnp.int32, (8, LANES), 0)
    zeros = jnp.zeros((K, LANES), jnp.float32)
    for piece in range(PIECES):
        leaf = leaves_ref[pl.ds(chunk * PIECES + piece, 1), :]
        sketch = stats_ref[piece * K : (piece + 1) * K, :]
        curve = stats_ref[PIECES * K + piece : PIECES * K + piece + 1, :]
        sketch = sketch.astype(jnp.bfloat16).astype(jnp.float32)
        curve = jnp.broadcast_to(curve, (8, LANES)).astype(jnp.bfloat16).astype(jnp.float32)
        masks = [jnp.broadcast_to(leaf == e, (K, LANES)) for e in range(LEAVES)]
        curve_mask = jnp.broadcast_to(leaf, (8, LANES)) == leaf_iota
        parts = [
            jnp.where(mask, term, zeros) for term in split_terms(sketch, SKETCH_SCALES) for mask in masks
        ]
        parts += [jnp.where(curve_mask, term, 0.0) for term in split_terms(curve, CURVE_SCALES)]
        parts.append(jnp.zeros((W_ROWS - 4 * TERM_ROWS - 16, LANES), jnp.float32))
        write(piece, jnp.concatenate(parts, axis=0).astype(F8))


def weight_kernel(ks, *refs):
    x = lax.axis_index("x").astype(jnp.int32)
    leaves_ref, out_ref = refs[-2:]
    for place, k in enumerate(ks):

        def write(piece, value, first=place * CHUNK):
            out_ref[:, first + piece * LANES : first + (piece + 1) * LANES] = value

        weight_block(refs[place], leaves_ref, x ^ k, write)


def weight_call(ks, stats, leaves):
    return pl.pallas_call(
        functools.partial(weight_kernel, ks),
        in_specs=[pl.BlockSpec(memory_space=pltpu.VMEM)] * (len(ks) + 1),
        out_specs=pl.BlockSpec(memory_space=pltpu.VMEM),
        out_shape=jax.ShapeDtypeStruct((W_ROWS, len(ks) * CHUNK), F8),
        compiler_params=pltpu.CompilerParams(vmem_limit_bytes=24 << 20),
        cost_estimate=pl.CostEstimate(flops=1_000_000, bytes_accessed=100_000, transcendentals=0),
        name="weights",
    )(*stats, leaves)


def count(codes, weights):
    codes = jnp.clip(codes, -1, OWN_BINS)
    pair = jnp.concatenate([codes, codes - 1], axis=0).astype(jnp.int8)
    one = jnp.ones(pair.shape, F8)
    zero = jnp.zeros(pair.shape, F8)
    onehot = jnp.concatenate(
        [jnp.where(pair == jnp.int8(b), one, zero) for b in range(0, OWN_BINS, 2)], axis=0
    )
    total = lax.dot_general(weights, onehot, NT, preferred_element_type=jnp.float32)
    sketch = sum(
        total[t * TERM_ROWS : (t + 1) * TERM_ROWS] * (1.0 / scale) for t, scale in enumerate(SKETCH_SCALES)
    )
    curve = sum(
        total[4 * TERM_ROWS + 8 * t : 4 * TERM_ROWS + 8 * t + 8] * (1.0 / scale)
        for t, scale in enumerate(CURVE_SCALES)
    )
    return jnp.concatenate(
        [sketch[:, :HALF], sketch[:, HALF:], curve[:LEAVES, :HALF], curve[:LEAVES, HALF:]], axis=0
    )


def first_bin(k, own):
    zl = lax.axis_index("zl").astype(jnp.int32)
    core = lax.axis_index("c").astype(jnp.int32)
    return OWN_BINS * (2 * (zl ^ k) + (core if own else 1 - core))


def block_bins(bins_ref, ks):
    x = lax.axis_index("x").astype(jnp.int32)
    return jnp.concatenate(
        [bins_ref[:, pl.ds(pl.multiple_of((x ^ k) * CHUNK, CHUNK), CHUNK)] for k in ks], axis=1
    )


def block_kernel(k, bins_ref, stats_ref, leaves_ref, *refs):
    out_ref, weights_ref = refs[-2:]
    weight_kernel((k,), stats_ref, leaves_ref, weights_ref)
    bins = block_bins(bins_ref, (k,))
    for to, own in ORDER:
        total = count(bins - first_bin(to, own), weights_ref[...])
        if len(refs) == 3:
            total += refs[0][4 * own + to]
        out_ref[4 * own + to] = total


def block_call(k, bins_t, stats, leaves, *before):
    return pl.pallas_call(
        functools.partial(block_kernel, k),
        in_specs=[pl.BlockSpec(memory_space=pltpu.VMEM)] * (3 + len(before)),
        out_specs=pl.BlockSpec(memory_space=pltpu.VMEM),
        out_shape=jax.ShapeDtypeStruct((8,) + PART, jnp.float32),
        scratch_shapes=[pltpu.VMEM((W_ROWS, CHUNK), F8)],
        compiler_params=pltpu.CompilerParams(vmem_limit_bytes=32 << 20),
        cost_estimate=pl.CostEstimate(flops=5_000_000_000, bytes_accessed=1_000_000, transcendentals=0),
        name="block",
    )(bins_t, stats, leaves, *before)


def other_kernel(ks, bins_ref, weights_ref, start_ref, out_ref):
    bins = block_bins(bins_ref, LAST)
    for place, k in enumerate(ks):
        out_ref[place] = start_ref[k] + count(bins - first_bin(k, False), weights_ref[...])


def other_call(ks, bins_t, weights, start):
    return pl.pallas_call(
        functools.partial(other_kernel, ks),
        in_specs=[pl.BlockSpec(memory_space=pltpu.VMEM)] * 3,
        out_specs=pl.BlockSpec(memory_space=pltpu.VMEM),
        out_shape=jax.ShapeDtypeStruct((len(ks),) + PART, jnp.float32),
        compiler_params=pltpu.CompilerParams(vmem_limit_bytes=32 << 20),
        cost_estimate=pl.CostEstimate(flops=OTHER_COST * len(ks), bytes_accessed=1000, transcendentals=0),
        name="other",
    )(bins_t, weights, start)


def hist_kernel(k, place, bins_ref, weights_ref, start_ref, swapped_ref, *refs):
    out_ref = refs[-1]
    bins = block_bins(bins_ref, LAST)
    total = start_ref[4 + k] + swapped_ref[place]
    for ref in refs[:-1]:
        total += ref[...]
    out_ref[...] = total + count(bins - first_bin(k, True), weights_ref[...])


def hist_call(k, bins_t, weights, start, swapped, place, *more):
    return pl.pallas_call(
        functools.partial(hist_kernel, k, place),
        in_specs=[pl.BlockSpec(memory_space=pltpu.VMEM)] * (4 + len(more)),
        out_specs=pl.BlockSpec(memory_space=pltpu.VMEM),
        out_shape=jax.ShapeDtypeStruct(PART, jnp.float32),
        compiler_params=pltpu.CompilerParams(vmem_limit_bytes=32 << 20),
        cost_estimate=pl.CostEstimate(flops=HIST_COST[k], bytes_accessed=1000, transcendentals=0),
        name="hist",
    )(bins_t, weights, start, swapped, *more)


def finish_kernel(a_ref, b_ref, out_ref):
    total = a_ref[...] + b_ref[...]
    for half in range(2):
        rows = []
        for e in range(LEAVES):
            first = half * TERM_ROWS + e * K
            rows.append(total[first : first + K])
            first = 2 * TERM_ROWS + half * LEAVES + e
            rows.append(total[first : first + 1])
        part = jnp.concatenate(rows, axis=0).T
        bins = OWN_BINS // 2
        out_ref[half * bins : (half + 1) * bins] = part.reshape(bins, FEATS, LEAVES * (K + 1))


def finish_call(parts):
    return pl.pallas_call(
        finish_kernel,
        out_shape=jax.ShapeDtypeStruct((OWN_BINS, FEATS, LEAVES * (K + 1)), jnp.float32),
        compiler_params=pltpu.CompilerParams(vmem_limit_bytes=8 << 20),
        name="finish",
    )(*parts)


def swap(value, axis, bit, size):
    return lax.ppermute(value, axis, [(i, i ^ bit) for i in range(size)])


def per_device(scores, targets, signs, bins, leaves):
    signs_t = signs.T
    bins_t = bins.T
    leaves2 = leaves.reshape(ROWS // LANES, LANES)

    (part,) = sketch_call((2,), scores, targets, signs_t)
    part, signs_t = lax.optimization_barrier((part, signs_t))
    first = swap(part, "x", 2, 4)
    parts = sketch_call((1, 3), scores, targets, signs_t)
    arrived = [swap(part, "x", k, 4) for k, part in zip((1, 3), parts)]
    (mine,) = sketch_call((0,), scores, targets, signs_t, first)
    mine = mine + (arrived[0] + arrived[1])
    arrived = [swap(mine, "y", k, 4) for k in (2, 1, 3)]
    mine = (mine + arrived[0]) + (arrived[1] + arrived[2])
    mine = mine + swap(mine, "zh", 1, 2)
    first = swap(mine, "x", 1, 4)
    last = [swap(mine, "x", k, 4) for k in LAST]
    start = block_call(0, bins_t, mine, leaves2)
    start = block_call(1, bins_t, first, leaves2, start)
    weights = weight_call(LAST, last, leaves2)

    far = swap(other_call((3,), bins_t, weights, start), "c", 1, 2)
    mid = other_call((2, 1), bins_t, weights, start)
    mid, start = lax.optimization_barrier((mid, start))
    mid = swap(mid, "c", 1, 2)
    part = hist_call(3, bins_t, weights, start, far, 0)
    part, start = lax.optimization_barrier((part, start))
    passed = swap(part, "zl", 1, 4)
    near = swap(other_call((0,), bins_t, weights, start), "c", 1, 2)
    moved1 = swap(hist_call(1, bins_t, weights, start, mid, 1), "zl", 1, 4)
    moved2 = swap(hist_call(2, bins_t, weights, start, mid, 0, passed), "zl", 2, 4)
    part = hist_call(0, bins_t, weights, start, near, 0, moved1)
    return finish_call((part, moved2))


def solution(mesh):
    fine = Mesh(mesh.devices.reshape(4, 2, 4, 4, 2), ("zl", "c", "y", "x", "zh"))
    row, lab = ("zl", "c"), ("y", "x", "zh")
    in_specs = (P(row, lab), P(row, lab), P(lab, None), P(row, lab), P(row))
    out_specs = P(row, lab, None)
    return jax.shard_map(
        per_device, mesh=fine, in_specs=in_specs, out_specs=out_specs, check_vma=False
    )
```

```python
import functools
import math

import jax
import jax.numpy as jnp
from jax import lax
from jax.experimental import pallas as pl
from jax.experimental.pallas import tpu as pltpu
from jax.sharding import Mesh, PartitionSpec as P

L = 8192
BINS = 256
K = 16
LEAVES = 4
ROWS = 8192
LABS = 256
FEATS = 16
SLAB = 512
LANES = 128
QUADS = SLAB // LANES
PIECES = 4 * QUADS
STAT_ROWS = PIECES * (K + 1)
F8 = jnp.float8_e4m3fn
NT = (((1,), (1,)), ((), ()))
SKETCH_SCALES = (4.0, 64.0, 2.0**24, 2.0**29)
CURVE_SCALES = (1024.0, 2.0**14)
TERM_ROWS = LEAVES * K
W_ROWS = 288
OWN_BINS = 32
CHUNK = 4 * SLAB
HALF = OWN_BINS * FEATS // 2
PART = (2 * LEAVES * (K + 1), HALF)
EARLY = ((3, False), (3, True), (2, False), (2, True))
MID_COST = 5_000_000_000
COST = 2_000_000_000
LAST = (3, 2)
GROUP = 4
SKETCH_VMEM = 51 << 20


def sketch_kernel(ks, scores_ref, targets_ref, signs_ref, *refs):
    more_refs, out_refs = refs[: -3 - len(ks)], refs[-3 - len(ks) : -3]
    score_buf, target_buf, sems = refs[-3:]
    x = lax.axis_index("x").astype(jnp.int32)

    def loads(slab):
        row = pl.multiple_of(((x ^ ks[slab // 4]) * 4 + slab % 4) * SLAB, SLAB)
        return (
            pltpu.make_async_copy(scores_ref.at[pl.ds(row, SLAB), :], score_buf.at[slab], sems.at[0, slab]),
            pltpu.make_async_copy(targets_ref.at[pl.ds(row, SLAB), :], target_buf.at[slab], sems.at[1, slab]),
        )

    for slab in range(4 * len(ks)):
        for copy in loads(slab):
            copy.start()
    sign_matrix = (2 * signs_ref[...] - 1).astype(jnp.bfloat16)
    left = jnp.concatenate(
        [
            jnp.concatenate([sign_matrix, sign_matrix, jnp.zeros((K, LABS), jnp.bfloat16)], axis=1),
            jnp.concatenate(
                [jnp.zeros((K, 2 * LABS), jnp.bfloat16), jnp.ones((K, LABS), jnp.bfloat16)], axis=1
            ),
        ],
        axis=0,
    )
    for first in range(0, 4 * len(ks), GROUP):
        for slab in range(first, first + GROUP):
            for copy in loads(slab):
                copy.wait()
        scores = score_buf[first : first + GROUP].reshape(GROUP * SLAB, LABS).astype(jnp.float32)
        targets = target_buf[first : first + GROUP].reshape(GROUP * SLAB, LABS).astype(jnp.float32)
        half_tanh = 0.5 * jnp.tanh(0.5 * scores)
        gradient = half_tanh + (0.5 - targets)
        hessian = 0.25 - half_tanh * half_tanh
        hessian = hessian[:, :LANES] + hessian[:, LANES:]
        grad_high = gradient.astype(jnp.bfloat16)
        grad_low = (gradient - grad_high.astype(jnp.float32)).astype(jnp.bfloat16)
        hess_high = hessian.astype(jnp.bfloat16)
        hess_low = (hessian - hess_high.astype(jnp.float32)).astype(jnp.bfloat16)
        right = jnp.concatenate([grad_high, grad_low, hess_high, hess_low], axis=1)
        stats = lax.dot_general(left, right, NT, preferred_element_type=jnp.float32)
        for piece in range(GROUP * QUADS):
            at, lanes = piece % PIECES, slice(piece * LANES, (piece + 1) * LANES)
            out_ref = out_refs[(first * QUADS + piece) // PIECES]
            rows, row = slice(at * K, (at + 1) * K), slice(PIECES * K + at, PIECES * K + at + 1)
            sketch = stats[:K, lanes] * (1.0 / math.sqrt(L))
            curve = stats[K : K + 1, lanes] * (1.0 / L)
            for more_ref in more_refs:
                sketch += more_ref[rows, :]
                curve += more_ref[row, :]
            out_ref[rows, :] = sketch
            out_ref[row, :] = curve


def sketch_call(ks, scores, targets, signs_t, *more):
    slabs = 4 * len(ks)
    return pl.pallas_call(
        functools.partial(sketch_kernel, ks),
        in_specs=[
            pl.BlockSpec(memory_space=pl.ANY),
            pl.BlockSpec(memory_space=pl.ANY),
        ]
        + [pl.BlockSpec(memory_space=pltpu.VMEM)] * (1 + len(more)),
        out_specs=[pl.BlockSpec(memory_space=pltpu.VMEM)] * len(ks),
        out_shape=[jax.ShapeDtypeStruct((STAT_ROWS, LANES), jnp.float32)] * len(ks),
        scratch_shapes=[
            pltpu.VMEM((slabs, SLAB, LABS), jnp.bfloat16),
            pltpu.VMEM((slabs, SLAB, LABS), jnp.int32),
            pltpu.SemaphoreType.DMA((2, slabs)),
        ],
        compiler_params=pltpu.CompilerParams(vmem_limit_bytes=SKETCH_VMEM),
        cost_estimate=pl.CostEstimate(
            flops=2 * slabs * SLAB * 768 * 32,
            bytes_accessed=slabs * SLAB * LABS * 6,
            transcendentals=slabs * SLAB * LABS,
        ),
        name="sketch",
    )(scores, targets, signs_t, *more)


def split_terms(values, scales):
    terms = []
    for scale in scales:
        term = (values * scale).astype(F8).astype(jnp.float32)
        terms.append(term)
        values = values - term * (1.0 / scale)
    return terms


def weight_block(stats_ref, leaves_ref, chunk, write):
    leaf_iota = lax.broadcasted_iota(jnp.int32, (8, LANES), 0)
    zeros = jnp.zeros((K, LANES), jnp.float32)
    for piece in range(PIECES):
        leaf = leaves_ref[pl.ds(chunk * PIECES + piece, 1), :]
        sketch = stats_ref[piece * K : (piece + 1) * K, :]
        curve = stats_ref[PIECES * K + piece : PIECES * K + piece + 1, :]
        sketch = sketch.astype(jnp.bfloat16).astype(jnp.float32)
        curve = jnp.broadcast_to(curve, (8, LANES)).astype(jnp.bfloat16).astype(jnp.float32)
        masks = [jnp.broadcast_to(leaf == e, (K, LANES)) for e in range(LEAVES)]
        curve_mask = jnp.broadcast_to(leaf, (8, LANES)) == leaf_iota
        parts = [
            jnp.where(mask, term, zeros) for term in split_terms(sketch, SKETCH_SCALES) for mask in masks
        ]
        parts += [jnp.where(curve_mask, term, 0.0) for term in split_terms(curve, CURVE_SCALES)]
        parts.append(jnp.zeros((W_ROWS - 4 * TERM_ROWS - 16, LANES), jnp.float32))
        write(piece, jnp.concatenate(parts, axis=0).astype(F8))


def weight_kernel(ks, *refs):
    x = lax.axis_index("x").astype(jnp.int32)
    leaves_ref, out_ref = refs[-2:]
    for place, k in enumerate(ks):

        def write(piece, value, first=place * CHUNK):
            out_ref[:, first + piece * LANES : first + (piece + 1) * LANES] = value

        weight_block(refs[place], leaves_ref, x ^ k, write)


def weight_call(ks, stats, leaves):
    return pl.pallas_call(
        functools.partial(weight_kernel, ks),
        in_specs=[pl.BlockSpec(memory_space=pltpu.VMEM)] * (len(ks) + 1),
        out_specs=pl.BlockSpec(memory_space=pltpu.VMEM),
        out_shape=jax.ShapeDtypeStruct((W_ROWS, len(ks) * CHUNK), F8),
        compiler_params=pltpu.CompilerParams(vmem_limit_bytes=24 << 20),
        cost_estimate=pl.CostEstimate(flops=1_000_000, bytes_accessed=100_000, transcendentals=0),
        name="weights",
    )(*stats, leaves)


def count(codes, weights):
    codes = jnp.clip(codes, -1, OWN_BINS)
    pair = jnp.concatenate([codes, codes - 1], axis=0).astype(jnp.int8)
    one = jnp.ones(pair.shape, F8)
    zero = jnp.zeros(pair.shape, F8)
    onehot = jnp.concatenate(
        [jnp.where(pair == jnp.int8(b), one, zero) for b in range(0, OWN_BINS, 2)], axis=0
    )
    return lax.dot_general(weights, onehot, NT, preferred_element_type=jnp.float32)


def combine(total):
    sketch = sum(
        total[t * TERM_ROWS : (t + 1) * TERM_ROWS] * (1.0 / scale) for t, scale in enumerate(SKETCH_SCALES)
    )
    curve = sum(
        total[4 * TERM_ROWS + 8 * t : 4 * TERM_ROWS + 8 * t + 8] * (1.0 / scale)
        for t, scale in enumerate(CURVE_SCALES)
    )
    return jnp.concatenate(
        [sketch[:, :HALF], sketch[:, HALF:], curve[:LEAVES, :HALF], curve[:LEAVES, HALF:]], axis=0
    )


def first_bin(k, own):
    zl = lax.axis_index("zl").astype(jnp.int32)
    core = lax.axis_index("c").astype(jnp.int32)
    return OWN_BINS * (2 * (zl ^ k) + (core if own else 1 - core))


def block_bins(bins_ref, ks):
    x = lax.axis_index("x").astype(jnp.int32)
    return jnp.concatenate(
        [bins_ref[:, pl.ds(pl.multiple_of((x ^ k) * CHUNK, CHUNK), CHUNK)] for k in ks], axis=1
    )


def block_kernel(k, bins_ref, stats_ref, leaves_ref, *refs):
    out_ref, weights_ref = refs[-2:]
    weight_kernel((k,), stats_ref, leaves_ref, weights_ref)
    bins = block_bins(bins_ref, (k,))
    for place, (to, own) in enumerate(EARLY):
        total = combine(count(bins - first_bin(to, own), weights_ref[...]))
        if len(refs) == 3:
            total += refs[0][place]
        out_ref[place] = total


def block_call(k, bins_t, stats, leaves, *before):
    return pl.pallas_call(
        functools.partial(block_kernel, k),
        in_specs=[pl.BlockSpec(memory_space=pltpu.VMEM)] * (3 + len(before)),
        out_specs=[pl.BlockSpec(memory_space=pltpu.VMEM)] * 2,
        out_shape=[
            jax.ShapeDtypeStruct((len(EARLY),) + PART, jnp.float32),
            jax.ShapeDtypeStruct((W_ROWS, CHUNK), F8),
        ],
        compiler_params=pltpu.CompilerParams(vmem_limit_bytes=32 << 20),
        cost_estimate=pl.CostEstimate(flops=5_000_000_000, bytes_accessed=1_000_000, transcendentals=0),
        name="block",
    )(bins_t, stats, leaves, *before)


def part_kernel(k, own, groups, bins_ref, *refs):
    out_ref = refs[-1]
    total = sum(
        count(block_bins(bins_ref, ks) - first_bin(k, own), ref[...]) for ks, ref in zip(groups, refs)
    )
    total = combine(total)
    for ref in refs[len(groups) : -1]:
        total += ref[EARLY.index((k, own))] if len(ref.shape) == 3 else ref[...]
    out_ref[...] = total


def part_call(k, own, bins_t, weights, *more, cost=1000):
    return pl.pallas_call(
        functools.partial(part_kernel, k, own, tuple(weights)),
        in_specs=[pl.BlockSpec(memory_space=pltpu.VMEM)] * (1 + len(weights) + len(more)),
        out_specs=pl.BlockSpec(memory_space=pltpu.VMEM),
        out_shape=jax.ShapeDtypeStruct(PART, jnp.float32),
        compiler_params=pltpu.CompilerParams(vmem_limit_bytes=32 << 20),
        cost_estimate=pl.CostEstimate(flops=cost, bytes_accessed=1000, transcendentals=0),
        name="own" if own else "other",
    )(bins_t, *weights.values(), *more)


def add_kernel(a_ref, b_ref, out_ref):
    out_ref[...] = a_ref[...] + b_ref[...]


def add_call(a, b):
    return pl.pallas_call(
        add_kernel,
        in_specs=[pl.BlockSpec(memory_space=pltpu.VMEM)] * 2,
        out_specs=pl.BlockSpec(memory_space=pltpu.VMEM),
        out_shape=jax.ShapeDtypeStruct(PART, jnp.float32),
        compiler_params=pltpu.CompilerParams(vmem_limit_bytes=8 << 20),
        cost_estimate=pl.CostEstimate(flops=MID_COST, bytes_accessed=1000, transcendentals=0),
        name="add",
    )(a, b)


def finish_kernel(a_ref, b_ref, out_ref):
    total = a_ref[...] + b_ref[...]
    for half in range(2):
        rows = []
        for e in range(LEAVES):
            first = half * TERM_ROWS + e * K
            rows.append(total[first : first + K])
            first = 2 * TERM_ROWS + half * LEAVES + e
            rows.append(total[first : first + 1])
        part = jnp.concatenate(rows, axis=0).T
        bins = OWN_BINS // 2
        out_ref[half * bins : (half + 1) * bins] = part.reshape(bins, FEATS, LEAVES * (K + 1))


def finish_call(parts):
    return pl.pallas_call(
        finish_kernel,
        out_shape=jax.ShapeDtypeStruct((OWN_BINS, FEATS, LEAVES * (K + 1)), jnp.float32),
        compiler_params=pltpu.CompilerParams(vmem_limit_bytes=8 << 20),
        name="finish",
    )(*parts)


def swap(value, axis, bit, size):
    return lax.ppermute(value, axis, [(i, i ^ bit) for i in range(size)])


def per_device(scores, targets, signs, bins, leaves):
    signs_t = signs.T
    bins_t = bins.T
    leaves2 = leaves.reshape(ROWS // LANES, LANES)

    (part,) = sketch_call((2,), scores, targets, signs_t)
    part, signs_t = lax.optimization_barrier((part, signs_t))
    first = swap(part, "x", 2, 4)
    parts = sketch_call((1, 3), scores, targets, signs_t)
    arrived = [swap(part, "x", k, 4) for k, part in zip((1, 3), parts)]
    (mine,) = sketch_call((0,), scores, targets, signs_t, first)
    mine = mine + (arrived[0] + arrived[1])
    arrived = [swap(mine, "y", k, 4) for k in (2, 1, 3)]
    mine = (mine + arrived[0]) + (arrived[1] + arrived[2])
    mine = mine + swap(mine, "zh", 1, 2)
    first = swap(mine, "x", 1, 4)
    last = [swap(mine, "x", k, 4) for k in LAST]
    start, weights0 = block_call(0, bins_t, mine, leaves2)
    start, weights1 = block_call(1, bins_t, first, leaves2, start)
    weights = weight_call(LAST, last, leaves2)

    rest = {LAST: weights}
    far = swap(part_call(3, False, bins_t, rest, start, cost=COST), "c", 1, 2)
    mid = part_call(2, False, bins_t, rest, start, cost=COST)
    mid, start = lax.optimization_barrier((mid, start))
    mid = swap(mid, "c", 1, 2)
    part = part_call(3, True, bins_t, rest, start, far)
    part, weights = lax.optimization_barrier((part, weights))
    passed = swap(part, "zl", 1, 4)
    whole = {(0,): weights0, (1,): weights1, LAST: weights}
    near = swap(part_call(1, False, bins_t, whole, cost=COST), "c", 1, 2)
    home = swap(part_call(0, False, bins_t, whole, cost=COST), "c", 1, 2)
    part = part_call(2, True, bins_t, rest, start, mid, passed, cost=MID_COST)
    part, weights = lax.optimization_barrier((part, weights))
    moved2 = swap(part, "zl", 2, 4)
    whole = {(0,): weights0, (1,): weights1, LAST: weights}
    moved1 = swap(part_call(1, True, bins_t, whole, near), "zl", 1, 4)
    part = part_call(0, True, bins_t, whole, home)
    return finish_call((add_call(part, moved2), moved1))


def solution(mesh):
    fine = Mesh(mesh.devices.reshape(4, 2, 4, 4, 2), ("zl", "c", "y", "x", "zh"))
    row, lab = ("zl", "c"), ("y", "x", "zh")
    in_specs = (P(row, lab), P(row, lab), P(lab, None), P(row, lab), P(row))
    out_specs = P(row, lab, None)
    return jax.shard_map(
        per_device, mesh=fine, in_specs=in_specs, out_specs=out_specs, check_vma=False
    )
```

```python
import functools
import math

import jax
import jax.numpy as jnp
from jax import lax
from jax.experimental import pallas as pl
from jax.experimental.pallas import tpu as pltpu
from jax.sharding import Mesh, PartitionSpec as P

L = 8192
BINS = 256
K = 16
LEAVES = 4
ROWS = 8192
LABS = 256
FEATS = 16
SLAB = 512
LANES = 128
QUADS = SLAB // LANES
PIECES = 4 * QUADS
STAT_ROWS = PIECES * (K + 1)
F8 = jnp.float8_e4m3fn
NT = (((1,), (1,)), ((), ()))
SKETCH_SCALES = (4.0, 64.0, 2.0**24, 2.0**29)
CURVE_SCALES = (1024.0, 2.0**14)
TERM_ROWS = LEAVES * K
W_ROWS = 288
OWN_BINS = 32
CHUNK = 4 * SLAB
HALF = OWN_BINS * FEATS // 2
PART = (2 * LEAVES * (K + 1), HALF)
EARLY = tuple((k, own) for k in (3, 2, 1) for own in (False, True))
CUT = LEAVES * K
MID_COST = 5_000_000_000
ADD_COSTS = (200_000_000, MID_COST)
COST = 1000
LAST = (3, 2)
GROUP = 4
SKETCH_VMEM = 51 << 20


def sketch_kernel(ks, scores_ref, targets_ref, signs_ref, *refs):
    more_refs, out_refs = refs[: -3 - len(ks)], refs[-3 - len(ks) : -3]
    score_buf, target_buf, sems = refs[-3:]
    x = lax.axis_index("x").astype(jnp.int32)

    def loads(slab):
        row = pl.multiple_of(((x ^ ks[slab // 4]) * 4 + slab % 4) * SLAB, SLAB)
        return (
            pltpu.make_async_copy(scores_ref.at[pl.ds(row, SLAB), :], score_buf.at[slab], sems.at[0, slab]),
            pltpu.make_async_copy(targets_ref.at[pl.ds(row, SLAB), :], target_buf.at[slab], sems.at[1, slab]),
        )

    for slab in range(4 * len(ks)):
        for copy in loads(slab):
            copy.start()
    sign_matrix = (2 * signs_ref[...] - 1).astype(jnp.bfloat16)
    left = jnp.concatenate(
        [
            jnp.concatenate([sign_matrix, sign_matrix, jnp.zeros((K, LABS), jnp.bfloat16)], axis=1),
            jnp.concatenate(
                [jnp.zeros((K, 2 * LABS), jnp.bfloat16), jnp.ones((K, LABS), jnp.bfloat16)], axis=1
            ),
        ],
        axis=0,
    )
    for first in range(0, 4 * len(ks), GROUP):
        for slab in range(first, first + GROUP):
            for copy in loads(slab):
                copy.wait()
        scores = score_buf[first : first + GROUP].reshape(GROUP * SLAB, LABS).astype(jnp.float32)
        targets = target_buf[first : first + GROUP].reshape(GROUP * SLAB, LABS).astype(jnp.float32)
        half_tanh = 0.5 * jnp.tanh(0.5 * scores)
        gradient = half_tanh + (0.5 - targets)
        hessian = 0.25 - half_tanh * half_tanh
        hessian = hessian[:, :LANES] + hessian[:, LANES:]
        grad_high = gradient.astype(jnp.bfloat16)
        grad_low = (gradient - grad_high.astype(jnp.float32)).astype(jnp.bfloat16)
        hess_high = hessian.astype(jnp.bfloat16)
        hess_low = (hessian - hess_high.astype(jnp.float32)).astype(jnp.bfloat16)
        right = jnp.concatenate([grad_high, grad_low, hess_high, hess_low], axis=1)
        stats = lax.dot_general(left, right, NT, preferred_element_type=jnp.float32)
        for piece in range(GROUP * QUADS):
            at, lanes = piece % PIECES, slice(piece * LANES, (piece + 1) * LANES)
            out_ref = out_refs[(first * QUADS + piece) // PIECES]
            rows, row = slice(at * K, (at + 1) * K), slice(PIECES * K + at, PIECES * K + at + 1)
            sketch = stats[:K, lanes] * (1.0 / math.sqrt(L))
            curve = stats[K : K + 1, lanes] * (1.0 / L)
            for more_ref in more_refs:
                sketch += more_ref[rows, :]
                curve += more_ref[row, :]
            out_ref[rows, :] = sketch
            out_ref[row, :] = curve


def sketch_call(ks, scores, targets, signs_t, *more):
    slabs = 4 * len(ks)
    return pl.pallas_call(
        functools.partial(sketch_kernel, ks),
        in_specs=[
            pl.BlockSpec(memory_space=pl.ANY),
            pl.BlockSpec(memory_space=pl.ANY),
        ]
        + [pl.BlockSpec(memory_space=pltpu.VMEM)] * (1 + len(more)),
        out_specs=[pl.BlockSpec(memory_space=pltpu.VMEM)] * len(ks),
        out_shape=[jax.ShapeDtypeStruct((STAT_ROWS, LANES), jnp.float32)] * len(ks),
        scratch_shapes=[
            pltpu.VMEM((slabs, SLAB, LABS), jnp.bfloat16),
            pltpu.VMEM((slabs, SLAB, LABS), jnp.int32),
            pltpu.SemaphoreType.DMA((2, slabs)),
        ],
        compiler_params=pltpu.CompilerParams(vmem_limit_bytes=SKETCH_VMEM),
        cost_estimate=pl.CostEstimate(
            flops=2 * slabs * SLAB * 768 * 32,
            bytes_accessed=slabs * SLAB * LABS * 6,
            transcendentals=slabs * SLAB * LABS,
        ),
        name="sketch",
    )(scores, targets, signs_t, *more)


def split_terms(values, scales):
    terms = []
    for scale in scales:
        term = (values * scale).astype(F8).astype(jnp.float32)
        terms.append(term)
        values = values - term * (1.0 / scale)
    return terms


def weight_block(stats_ref, leaves_ref, chunk, write):
    leaf_iota = lax.broadcasted_iota(jnp.int32, (8, LANES), 0)
    zeros = jnp.zeros((K, LANES), jnp.float32)
    for piece in range(PIECES):
        leaf = leaves_ref[pl.ds(chunk * PIECES + piece, 1), :]
        sketch = stats_ref[piece * K : (piece + 1) * K, :]
        curve = stats_ref[PIECES * K + piece : PIECES * K + piece + 1, :]
        sketch = sketch.astype(jnp.bfloat16).astype(jnp.float32)
        curve = jnp.broadcast_to(curve, (8, LANES)).astype(jnp.bfloat16).astype(jnp.float32)
        masks = [jnp.broadcast_to(leaf == e, (K, LANES)) for e in range(LEAVES)]
        curve_mask = jnp.broadcast_to(leaf, (8, LANES)) == leaf_iota
        parts = [
            jnp.where(mask, term, zeros) for term in split_terms(sketch, SKETCH_SCALES) for mask in masks
        ]
        parts += [jnp.where(curve_mask, term, 0.0) for term in split_terms(curve, CURVE_SCALES)]
        parts.append(jnp.zeros((W_ROWS - 4 * TERM_ROWS - 16, LANES), jnp.float32))
        write(piece, jnp.concatenate(parts, axis=0).astype(F8))


def weight_kernel(ks, *refs):
    x = lax.axis_index("x").astype(jnp.int32)
    leaves_ref, out_ref = refs[-2:]
    for place, k in enumerate(ks):

        def write(piece, value, first=place * CHUNK):
            out_ref[:, first + piece * LANES : first + (piece + 1) * LANES] = value

        weight_block(refs[place], leaves_ref, x ^ k, write)


def weight_call(ks, stats, leaves):
    return pl.pallas_call(
        functools.partial(weight_kernel, ks),
        in_specs=[pl.BlockSpec(memory_space=pltpu.VMEM)] * (len(ks) + 1),
        out_specs=pl.BlockSpec(memory_space=pltpu.VMEM),
        out_shape=jax.ShapeDtypeStruct((W_ROWS, len(ks) * CHUNK), F8),
        compiler_params=pltpu.CompilerParams(vmem_limit_bytes=24 << 20),
        cost_estimate=pl.CostEstimate(flops=1_000_000, bytes_accessed=100_000, transcendentals=0),
        name="weights",
    )(*stats, leaves)


def count(codes, weights):
    codes = jnp.clip(codes, -1, OWN_BINS)
    pair = jnp.concatenate([codes, codes - 1], axis=0).astype(jnp.int8)
    one = jnp.ones(pair.shape, F8)
    zero = jnp.zeros(pair.shape, F8)
    onehot = jnp.concatenate(
        [jnp.where(pair == jnp.int8(b), one, zero) for b in range(0, OWN_BINS, 2)], axis=0
    )
    return lax.dot_general(weights, onehot, NT, preferred_element_type=jnp.float32)


def combine(total):
    sketch = sum(
        total[t * TERM_ROWS : (t + 1) * TERM_ROWS] * (1.0 / scale) for t, scale in enumerate(SKETCH_SCALES)
    )
    curve = sum(
        total[4 * TERM_ROWS + 8 * t : 4 * TERM_ROWS + 8 * t + 8] * (1.0 / scale)
        for t, scale in enumerate(CURVE_SCALES)
    )
    return jnp.concatenate(
        [sketch[:, :HALF], sketch[:, HALF:], curve[:LEAVES, :HALF], curve[:LEAVES, HALF:]], axis=0
    )


def first_bin(k, own):
    zl = lax.axis_index("zl").astype(jnp.int32)
    core = lax.axis_index("c").astype(jnp.int32)
    return OWN_BINS * (2 * (zl ^ k) + (core if own else 1 - core))


def block_bins(bins_ref, ks):
    x = lax.axis_index("x").astype(jnp.int32)
    return jnp.concatenate(
        [bins_ref[:, pl.ds(pl.multiple_of((x ^ k) * CHUNK, CHUNK), CHUNK)] for k in ks], axis=1
    )


def block_kernel(k, bins_ref, stats_ref, leaves_ref, *refs):
    out_ref, weights_ref = refs[-2:]
    weight_kernel((k,), stats_ref, leaves_ref, weights_ref)
    bins = block_bins(bins_ref, (k,))
    for place, (to, own) in enumerate(EARLY):
        total = combine(count(bins - first_bin(to, own), weights_ref[...]))
        if len(refs) == 3:
            total += refs[0][place]
        out_ref[place] = total


def block_call(k, bins_t, stats, leaves, *before):
    return pl.pallas_call(
        functools.partial(block_kernel, k),
        in_specs=[pl.BlockSpec(memory_space=pltpu.VMEM)] * (3 + len(before)),
        out_specs=[pl.BlockSpec(memory_space=pltpu.VMEM)] * 2,
        out_shape=[
            jax.ShapeDtypeStruct((len(EARLY),) + PART, jnp.float32),
            jax.ShapeDtypeStruct((W_ROWS, CHUNK), F8),
        ],
        compiler_params=pltpu.CompilerParams(vmem_limit_bytes=32 << 20),
        cost_estimate=pl.CostEstimate(flops=5_000_000_000, bytes_accessed=1_000_000, transcendentals=0),
        name="block",
    )(bins_t, stats, leaves, *before)


def part_kernel(k, own, groups, outs, bins_ref, *refs):
    total = sum(
        count(block_bins(bins_ref, ks) - first_bin(k, own), ref[...]) for ks, ref in zip(groups, refs)
    )
    total = combine(total)
    for ref in refs[len(groups) : -outs]:
        total += ref[EARLY.index((k, own))] if len(ref.shape) == 3 else ref[...]
    if outs == 1:
        refs[-1][...] = total
    else:
        refs[-2][...] = total[:CUT]
        refs[-1][...] = total[CUT:]


def part_call(k, own, bins_t, weights, *more, cut=False, cost=1000):
    shapes = [(CUT, PART[1]), (PART[0] - CUT, PART[1])] if cut else [PART]
    outs = pl.pallas_call(
        functools.partial(part_kernel, k, own, tuple(weights), len(shapes)),
        in_specs=[pl.BlockSpec(memory_space=pltpu.VMEM)] * (1 + len(weights) + len(more)),
        out_specs=[pl.BlockSpec(memory_space=pltpu.VMEM)] * len(shapes),
        out_shape=[jax.ShapeDtypeStruct(shape, jnp.float32) for shape in shapes],
        compiler_params=pltpu.CompilerParams(vmem_limit_bytes=32 << 20),
        cost_estimate=pl.CostEstimate(flops=cost, bytes_accessed=1000, transcendentals=0),
        name="own" if own else "other",
    )(bins_t, *weights.values(), *more)
    return outs if cut else outs[0]


def add_kernel(a_ref, b_ref, out_ref):
    out_ref[...] = a_ref[...] + b_ref[...]


def add_call(a, b, cost=1000):
    return pl.pallas_call(
        add_kernel,
        in_specs=[pl.BlockSpec(memory_space=pltpu.VMEM)] * 2,
        out_specs=pl.BlockSpec(memory_space=pltpu.VMEM),
        out_shape=jax.ShapeDtypeStruct(a.shape, jnp.float32),
        compiler_params=pltpu.CompilerParams(vmem_limit_bytes=8 << 20),
        cost_estimate=pl.CostEstimate(flops=cost, bytes_accessed=1000, transcendentals=0),
        name="add",
    )(a, b)


def finish_kernel(upper_ref, lower_ref, moved_ref, last_ref, out_ref):
    total = jnp.concatenate([upper_ref[...], lower_ref[...] + last_ref[...]], axis=0) + moved_ref[...]
    for half in range(2):
        rows = []
        for e in range(LEAVES):
            first = half * TERM_ROWS + e * K
            rows.append(total[first : first + K])
            first = 2 * TERM_ROWS + half * LEAVES + e
            rows.append(total[first : first + 1])
        part = jnp.concatenate(rows, axis=0).T
        bins = OWN_BINS // 2
        out_ref[half * bins : (half + 1) * bins] = part.reshape(bins, FEATS, LEAVES * (K + 1))


def finish_call(parts):
    return pl.pallas_call(
        finish_kernel,
        out_shape=jax.ShapeDtypeStruct((OWN_BINS, FEATS, LEAVES * (K + 1)), jnp.float32),
        compiler_params=pltpu.CompilerParams(vmem_limit_bytes=8 << 20),
        name="finish",
    )(*parts)


def swap(value, axis, bit, size):
    return lax.ppermute(value, axis, [(i, i ^ bit) for i in range(size)])


def per_device(scores, targets, signs, bins, leaves):
    signs_t = signs.T
    bins_t = bins.T
    leaves2 = leaves.reshape(ROWS // LANES, LANES)

    (part,) = sketch_call((2,), scores, targets, signs_t)
    part, signs_t = lax.optimization_barrier((part, signs_t))
    first = swap(part, "x", 2, 4)
    parts = sketch_call((1, 3), scores, targets, signs_t)
    arrived = [swap(part, "x", k, 4) for k, part in zip((1, 3), parts)]
    (mine,) = sketch_call((0,), scores, targets, signs_t, first)
    mine = mine + (arrived[0] + arrived[1])
    arrived = [swap(mine, "y", k, 4) for k in (2, 1, 3)]
    mine = (mine + arrived[0]) + (arrived[1] + arrived[2])
    mine = mine + swap(mine, "zh", 1, 2)
    first = swap(mine, "x", 1, 4)
    last = [swap(mine, "x", k, 4) for k in LAST]
    start, weights0 = block_call(0, bins_t, mine, leaves2)
    start, weights1 = block_call(1, bins_t, first, leaves2, start)
    weights = weight_call(LAST, last, leaves2)

    rest = {LAST: weights}
    far = swap(part_call(3, False, bins_t, rest, start, cost=COST), "c", 1, 2)
    mid = part_call(2, False, bins_t, rest, start, cost=COST)
    near = part_call(1, False, bins_t, rest, start, cost=COST)
    mid, near, start = lax.optimization_barrier((mid, near, start))
    mid, near = swap(mid, "c", 1, 2), swap(near, "c", 1, 2)
    upper, lower = part_call(3, True, bins_t, rest, start, far, cut=True)
    upper, lower, start, weights = lax.optimization_barrier((upper, lower, start, weights))
    passed = [swap(upper, "zl", 1, 4), swap(lower, "zl", 1, 4)]
    rest = {LAST: weights}
    moved1 = swap(part_call(1, True, bins_t, rest, start, near), "zl", 1, 4)
    upper, lower = part_call(2, True, bins_t, rest, start, mid, cut=True)
    upper, lower, weights = lax.optimization_barrier((upper, lower, weights))
    whole = {(0,): weights0, (1,): weights1, LAST: weights}
    moved2 = [swap(add_call(a, b, cost), "zl", 2, 4) for a, b, cost in zip((upper, lower), passed, ADD_COSTS)]
    home = swap(part_call(0, False, bins_t, whole, cost=COST), "c", 1, 2)
    upper, lower = part_call(0, True, bins_t, whole, home, cut=True)
    return finish_call((add_call(upper, moved2[0], MID_COST), lower, moved1, moved2[1]))


def solution(mesh):
    fine = Mesh(mesh.devices.reshape(4, 2, 4, 4, 2), ("zl", "c", "y", "x", "zh"))
    row, lab = ("zl", "c"), ("y", "x", "zh")
    in_specs = (P(row, lab), P(row, lab), P(lab, None), P(row, lab), P(row))
    out_specs = P(row, lab, None)
    return jax.shard_map(
        per_device, mesh=fine, in_specs=in_specs, out_specs=out_specs, check_vma=False
    )
```

```python
import functools
import math

import jax
import jax.numpy as jnp
from jax import lax
from jax.experimental import pallas as pl
from jax.experimental.pallas import tpu as pltpu
from jax.sharding import Mesh, PartitionSpec as P

L = 8192
BINS = 256
K = 16
LEAVES = 4
ROWS = 8192
LABS = 256
FEATS = 16
SLAB = 512
LANES = 128
QUADS = SLAB // LANES
PIECES = 4 * QUADS
STAT_ROWS = PIECES * (K + 1)
F8 = jnp.float8_e4m3fn
NT = (((1,), (1,)), ((), ()))
SKETCH_SCALES = (4.0, 64.0, 2.0**24, 2.0**29)
CURVE_SCALES = (1024.0, 2.0**14)
TERM_ROWS = LEAVES * K
W_ROWS = 288
OWN_BINS = 32
CHUNK = 4 * SLAB
HALF = OWN_BINS * FEATS // 2
PART = (2 * LEAVES * (K + 1), HALF)
ORDER = tuple((k, own) for k in (3, 2, 1, 0) for own in (False, True))
OTHER_COST = 2_000_000_000
HIST_COST = (1000, 1000, 1000, 1000)
ADD_COST = 5_000_000_000
LAST = (3, 2)
GROUP = 4
SKETCH_VMEM = 51 << 20


def sketch_kernel(ks, scores_ref, targets_ref, signs_ref, *refs):
    more_refs, out_refs = refs[: -3 - len(ks)], refs[-3 - len(ks) : -3]
    score_buf, target_buf, sems = refs[-3:]
    x = lax.axis_index("x").astype(jnp.int32)

    def loads(slab):
        row = pl.multiple_of(((x ^ ks[slab // 4]) * 4 + slab % 4) * SLAB, SLAB)
        return (
            pltpu.make_async_copy(scores_ref.at[pl.ds(row, SLAB), :], score_buf.at[slab], sems.at[0, slab]),
            pltpu.make_async_copy(targets_ref.at[pl.ds(row, SLAB), :], target_buf.at[slab], sems.at[1, slab]),
        )

    for slab in range(4 * len(ks)):
        for copy in loads(slab):
            copy.start()
    sign_matrix = (2 * signs_ref[...] - 1).astype(jnp.bfloat16)
    left = jnp.concatenate(
        [
            jnp.concatenate([sign_matrix, sign_matrix, jnp.zeros((K, LABS), jnp.bfloat16)], axis=1),
            jnp.concatenate(
                [jnp.zeros((K, 2 * LABS), jnp.bfloat16), jnp.ones((K, LABS), jnp.bfloat16)], axis=1
            ),
        ],
        axis=0,
    )
    for first in range(0, 4 * len(ks), GROUP):
        for slab in range(first, first + GROUP):
            for copy in loads(slab):
                copy.wait()
        scores = score_buf[first : first + GROUP].reshape(GROUP * SLAB, LABS).astype(jnp.float32)
        targets = target_buf[first : first + GROUP].reshape(GROUP * SLAB, LABS).astype(jnp.float32)
        half_tanh = 0.5 * jnp.tanh(0.5 * scores)
        gradient = half_tanh + (0.5 - targets)
        hessian = 0.25 - half_tanh * half_tanh
        hessian = hessian[:, :LANES] + hessian[:, LANES:]
        grad_high = gradient.astype(jnp.bfloat16)
        grad_low = (gradient - grad_high.astype(jnp.float32)).astype(jnp.bfloat16)
        hess_high = hessian.astype(jnp.bfloat16)
        hess_low = (hessian - hess_high.astype(jnp.float32)).astype(jnp.bfloat16)
        right = jnp.concatenate([grad_high, grad_low, hess_high, hess_low], axis=1)
        stats = lax.dot_general(left, right, NT, preferred_element_type=jnp.float32)
        for piece in range(GROUP * QUADS):
            at, lanes = piece % PIECES, slice(piece * LANES, (piece + 1) * LANES)
            out_ref = out_refs[(first * QUADS + piece) // PIECES]
            rows, row = slice(at * K, (at + 1) * K), slice(PIECES * K + at, PIECES * K + at + 1)
            sketch = stats[:K, lanes] * (1.0 / math.sqrt(L))
            curve = stats[K : K + 1, lanes] * (1.0 / L)
            for more_ref in more_refs:
                sketch += more_ref[rows, :]
                curve += more_ref[row, :]
            out_ref[rows, :] = sketch
            out_ref[row, :] = curve


def sketch_call(ks, scores, targets, signs_t, *more):
    slabs = 4 * len(ks)
    return pl.pallas_call(
        functools.partial(sketch_kernel, ks),
        in_specs=[
            pl.BlockSpec(memory_space=pl.ANY),
            pl.BlockSpec(memory_space=pl.ANY),
        ]
        + [pl.BlockSpec(memory_space=pltpu.VMEM)] * (1 + len(more)),
        out_specs=[pl.BlockSpec(memory_space=pltpu.VMEM)] * len(ks),
        out_shape=[jax.ShapeDtypeStruct((STAT_ROWS, LANES), jnp.float32)] * len(ks),
        scratch_shapes=[
            pltpu.VMEM((slabs, SLAB, LABS), jnp.bfloat16),
            pltpu.VMEM((slabs, SLAB, LABS), jnp.int32),
            pltpu.SemaphoreType.DMA((2, slabs)),
        ],
        compiler_params=pltpu.CompilerParams(vmem_limit_bytes=SKETCH_VMEM),
        cost_estimate=pl.CostEstimate(
            flops=2 * slabs * SLAB * 768 * 32,
            bytes_accessed=slabs * SLAB * LABS * 6,
            transcendentals=slabs * SLAB * LABS,
        ),
        name="sketch",
    )(scores, targets, signs_t, *more)


def split_terms(values, scales):
    terms = []
    for scale in scales:
        term = (values * scale).astype(F8).astype(jnp.float32)
        terms.append(term)
        values = values - term * (1.0 / scale)
    return terms


def weight_block(stats_ref, leaves_ref, chunk, write):
    leaf_iota = lax.broadcasted_iota(jnp.int32, (8, LANES), 0)
    zeros = jnp.zeros((K, LANES), jnp.float32)
    for piece in range(PIECES):
        leaf = leaves_ref[pl.ds(chunk * PIECES + piece, 1), :]
        sketch = stats_ref[piece * K : (piece + 1) * K, :]
        curve = stats_ref[PIECES * K + piece : PIECES * K + piece + 1, :]
        sketch = sketch.astype(jnp.bfloat16).astype(jnp.float32)
        curve = jnp.broadcast_to(curve, (8, LANES)).astype(jnp.bfloat16).astype(jnp.float32)
        masks = [jnp.broadcast_to(leaf == e, (K, LANES)) for e in range(LEAVES)]
        curve_mask = jnp.broadcast_to(leaf, (8, LANES)) == leaf_iota
        parts = [
            jnp.where(mask, term, zeros) for term in split_terms(sketch, SKETCH_SCALES) for mask in masks
        ]
        parts += [jnp.where(curve_mask, term, 0.0) for term in split_terms(curve, CURVE_SCALES)]
        parts.append(jnp.zeros((W_ROWS - 4 * TERM_ROWS - 16, LANES), jnp.float32))
        write(piece, jnp.concatenate(parts, axis=0).astype(F8))


def weight_kernel(ks, *refs):
    x = lax.axis_index("x").astype(jnp.int32)
    leaves_ref, out_ref = refs[-2:]
    for place, k in enumerate(ks):

        def write(piece, value, first=place * CHUNK):
            out_ref[:, first + piece * LANES : first + (piece + 1) * LANES] = value

        weight_block(refs[place], leaves_ref, x ^ k, write)


def weight_call(ks, stats, leaves):
    return pl.pallas_call(
        functools.partial(weight_kernel, ks),
        in_specs=[pl.BlockSpec(memory_space=pltpu.VMEM)] * (len(ks) + 1),
        out_specs=pl.BlockSpec(memory_space=pltpu.VMEM),
        out_shape=jax.ShapeDtypeStruct((W_ROWS, len(ks) * CHUNK), F8),
        compiler_params=pltpu.CompilerParams(vmem_limit_bytes=24 << 20),
        cost_estimate=pl.CostEstimate(flops=1_000_000, bytes_accessed=100_000, transcendentals=0),
        name="weights",
    )(*stats, leaves)


def count(codes, weights):
    codes = jnp.clip(codes, -1, OWN_BINS)
    pair = jnp.concatenate([codes, codes - 1], axis=0).astype(jnp.int8)
    one = jnp.ones(pair.shape, F8)
    zero = jnp.zeros(pair.shape, F8)
    onehot = jnp.concatenate(
        [jnp.where(pair == jnp.int8(b), one, zero) for b in range(0, OWN_BINS, 2)], axis=0
    )
    total = lax.dot_general(weights, onehot, NT, preferred_element_type=jnp.float32)
    sketch = sum(
        total[t * TERM_ROWS : (t + 1) * TERM_ROWS] * (1.0 / scale) for t, scale in enumerate(SKETCH_SCALES)
    )
    curve = sum(
        total[4 * TERM_ROWS + 8 * t : 4 * TERM_ROWS + 8 * t + 8] * (1.0 / scale)
        for t, scale in enumerate(CURVE_SCALES)
    )
    return jnp.concatenate(
        [sketch[:, :HALF], sketch[:, HALF:], curve[:LEAVES, :HALF], curve[:LEAVES, HALF:]], axis=0
    )


def first_bin(k, own):
    zl = lax.axis_index("zl").astype(jnp.int32)
    core = lax.axis_index("c").astype(jnp.int32)
    return OWN_BINS * (2 * (zl ^ k) + (core if own else 1 - core))


def block_bins(bins_ref, ks):
    x = lax.axis_index("x").astype(jnp.int32)
    return jnp.concatenate(
        [bins_ref[:, pl.ds(pl.multiple_of((x ^ k) * CHUNK, CHUNK), CHUNK)] for k in ks], axis=1
    )


def block_kernel(k, bins_ref, stats_ref, leaves_ref, *refs):
    out_ref, weights_ref = refs[-2:]
    weight_kernel((k,), stats_ref, leaves_ref, weights_ref)
    bins = block_bins(bins_ref, (k,))
    for to, own in ORDER:
        total = count(bins - first_bin(to, own), weights_ref[...])
        if len(refs) == 3:
            total += refs[0][4 * own + to]
        out_ref[4 * own + to] = total


def block_call(k, bins_t, stats, leaves, *before):
    return pl.pallas_call(
        functools.partial(block_kernel, k),
        in_specs=[pl.BlockSpec(memory_space=pltpu.VMEM)] * (3 + len(before)),
        out_specs=pl.BlockSpec(memory_space=pltpu.VMEM),
        out_shape=jax.ShapeDtypeStruct((8,) + PART, jnp.float32),
        scratch_shapes=[pltpu.VMEM((W_ROWS, CHUNK), F8)],
        compiler_params=pltpu.CompilerParams(vmem_limit_bytes=32 << 20),
        cost_estimate=pl.CostEstimate(flops=5_000_000_000, bytes_accessed=1_000_000, transcendentals=0),
        name="block",
    )(bins_t, stats, leaves, *before)


def other_kernel(ks, bins_ref, weights_ref, start_ref, out_ref):
    bins = block_bins(bins_ref, LAST)
    for place, k in enumerate(ks):
        out_ref[place] = start_ref[k] + count(bins - first_bin(k, False), weights_ref[...])


def other_call(ks, bins_t, weights, start):
    return pl.pallas_call(
        functools.partial(other_kernel, ks),
        in_specs=[pl.BlockSpec(memory_space=pltpu.VMEM)] * 3,
        out_specs=pl.BlockSpec(memory_space=pltpu.VMEM),
        out_shape=jax.ShapeDtypeStruct((len(ks),) + PART, jnp.float32),
        compiler_params=pltpu.CompilerParams(vmem_limit_bytes=32 << 20),
        cost_estimate=pl.CostEstimate(flops=OTHER_COST * len(ks), bytes_accessed=1000, transcendentals=0),
        name="other",
    )(bins_t, weights, start)


def hist_kernel(k, place, bins_ref, weights_ref, start_ref, swapped_ref, *refs):
    out_ref = refs[-1]
    bins = block_bins(bins_ref, LAST)
    total = start_ref[4 + k] + swapped_ref[place]
    for ref in refs[:-1]:
        total += ref[...]
    out_ref[...] = total + count(bins - first_bin(k, True), weights_ref[...])


def hist_call(k, bins_t, weights, start, swapped, place, *more):
    return pl.pallas_call(
        functools.partial(hist_kernel, k, place),
        in_specs=[pl.BlockSpec(memory_space=pltpu.VMEM)] * (4 + len(more)),
        out_specs=pl.BlockSpec(memory_space=pltpu.VMEM),
        out_shape=jax.ShapeDtypeStruct(PART, jnp.float32),
        compiler_params=pltpu.CompilerParams(vmem_limit_bytes=32 << 20),
        cost_estimate=pl.CostEstimate(flops=HIST_COST[k], bytes_accessed=1000, transcendentals=0),
        name="hist",
    )(bins_t, weights, start, swapped, *more)


def add_kernel(a_ref, b_ref, out_ref):
    out_ref[...] = a_ref[...] + b_ref[...]


def add_call(a, b):
    return pl.pallas_call(
        add_kernel,
        in_specs=[pl.BlockSpec(memory_space=pltpu.VMEM)] * 2,
        out_specs=pl.BlockSpec(memory_space=pltpu.VMEM),
        out_shape=jax.ShapeDtypeStruct(PART, jnp.float32),
        compiler_params=pltpu.CompilerParams(vmem_limit_bytes=8 << 20),
        cost_estimate=pl.CostEstimate(flops=ADD_COST, bytes_accessed=1000, transcendentals=0),
        name="add",
    )(a, b)


def finish_kernel(a_ref, b_ref, out_ref):
    total = a_ref[...] + b_ref[...]
    for half in range(2):
        rows = []
        for e in range(LEAVES):
            first = half * TERM_ROWS + e * K
            rows.append(total[first : first + K])
            first = 2 * TERM_ROWS + half * LEAVES + e
            rows.append(total[first : first + 1])
        part = jnp.concatenate(rows, axis=0).T
        bins = OWN_BINS // 2
        out_ref[half * bins : (half + 1) * bins] = part.reshape(bins, FEATS, LEAVES * (K + 1))


def finish_call(parts):
    return pl.pallas_call(
        finish_kernel,
        out_shape=jax.ShapeDtypeStruct((OWN_BINS, FEATS, LEAVES * (K + 1)), jnp.float32),
        compiler_params=pltpu.CompilerParams(vmem_limit_bytes=8 << 20),
        name="finish",
    )(*parts)


def swap(value, axis, bit, size):
    return lax.ppermute(value, axis, [(i, i ^ bit) for i in range(size)])


def per_device(scores, targets, signs, bins, leaves):
    signs_t = signs.T
    bins_t = bins.T
    leaves2 = leaves.reshape(ROWS // LANES, LANES)

    (part,) = sketch_call((2,), scores, targets, signs_t)
    part, signs_t = lax.optimization_barrier((part, signs_t))
    first = swap(part, "x", 2, 4)
    parts = sketch_call((1, 3), scores, targets, signs_t)
    arrived = [swap(part, "x", k, 4) for k, part in zip((1, 3), parts)]
    (mine,) = sketch_call((0,), scores, targets, signs_t, first)
    mine = mine + (arrived[0] + arrived[1])
    arrived = [swap(mine, "y", k, 4) for k in (2, 1, 3)]
    mine = (mine + arrived[0]) + (arrived[1] + arrived[2])
    mine = mine + swap(mine, "zh", 1, 2)
    first = swap(mine, "x", 1, 4)
    last = [swap(mine, "x", k, 4) for k in LAST]
    start = block_call(0, bins_t, mine, leaves2)
    start = block_call(1, bins_t, first, leaves2, start)
    weights = weight_call(LAST, last, leaves2)

    far = swap(other_call((3,), bins_t, weights, start), "c", 1, 2)
    mid = other_call((2,), bins_t, weights, start)
    mid, start = lax.optimization_barrier((mid, start))
    mid = swap(mid, "c", 1, 2)
    part = hist_call(3, bins_t, weights, start, far, 0)
    part, start = lax.optimization_barrier((part, start))
    passed = swap(part, "zl", 1, 4)
    near = swap(other_call((1,), bins_t, weights, start), "c", 1, 2)
    part = hist_call(2, bins_t, weights, start, mid, 0)
    moved1 = swap(hist_call(1, bins_t, weights, start, near, 0), "zl", 1, 4)
    moved2 = swap(add_call(part, passed), "zl", 2, 4)
    home = swap(other_call((0,), bins_t, weights, start), "c", 1, 2)
    part = hist_call(0, bins_t, weights, start, home, 0, moved1)
    return finish_call((part, moved2))


def solution(mesh):
    fine = Mesh(mesh.devices.reshape(4, 2, 4, 4, 2), ("zl", "c", "y", "x", "zh"))
    row, lab = ("zl", "c"), ("y", "x", "zh")
    in_specs = (P(row, lab), P(row, lab), P(lab, None), P(row, lab), P(row))
    out_specs = P(row, lab, None)
    return jax.shard_map(
        per_device, mesh=fine, in_specs=in_specs, out_specs=out_specs, check_vma=False
    )
```

```python
import functools
import math

import jax
import jax.numpy as jnp
from jax import lax
from jax.experimental import pallas as pl
from jax.experimental.pallas import tpu as pltpu
from jax.sharding import Mesh, PartitionSpec as P

L = 8192
BINS = 256
K = 16
LEAVES = 4
ROWS = 8192
LABS = 256
FEATS = 16
SLAB = 512
LANES = 128
QUADS = SLAB // LANES
PIECES = 4 * QUADS
STAT_ROWS = PIECES * (K + 1)
F8 = jnp.float8_e4m3fn
NT = (((1,), (1,)), ((), ()))
SKETCH_SCALES = (4.0, 64.0, 2.0**24, 2.0**29)
CURVE_SCALES = (1024.0, 2.0**14)
TERM_ROWS = LEAVES * K
W_ROWS = 288
OWN_BINS = 32
CHUNK = 4 * SLAB
HALF = OWN_BINS * FEATS // 2
PART = (2 * LEAVES * (K + 1), HALF)
ORDER = tuple((k, own) for k in (3, 2, 1, 0) for own in (False, True))
OTHER_COST = 2_000_000_000
HIST_COST = (1000, 1000, 1000, 1000)
ADD_COST = 5_000_000_000
LAST = (3, 2)
GROUP = 4
SKETCH_VMEM = 51 << 20


def sketch_kernel(ks, scores_ref, targets_ref, signs_ref, *refs):
    more_refs, out_refs = refs[: -3 - len(ks)], refs[-3 - len(ks) : -3]
    score_buf, target_buf, sems = refs[-3:]
    x = lax.axis_index("x").astype(jnp.int32)

    def loads(slab):
        row = pl.multiple_of(((x ^ ks[slab // 4]) * 4 + slab % 4) * SLAB, SLAB)
        return (
            pltpu.make_async_copy(scores_ref.at[pl.ds(row, SLAB), :], score_buf.at[slab], sems.at[0, slab]),
            pltpu.make_async_copy(targets_ref.at[pl.ds(row, SLAB), :], target_buf.at[slab], sems.at[1, slab]),
        )

    for slab in range(4 * len(ks)):
        for copy in loads(slab):
            copy.start()
    sign_matrix = (2 * signs_ref[...] - 1).astype(jnp.bfloat16)
    left = jnp.concatenate(
        [
            jnp.concatenate([sign_matrix, sign_matrix, jnp.zeros((K, LABS), jnp.bfloat16)], axis=1),
            jnp.concatenate(
                [jnp.zeros((K, 2 * LABS), jnp.bfloat16), jnp.ones((K, LABS), jnp.bfloat16)], axis=1
            ),
        ],
        axis=0,
    )
    for first in range(0, 4 * len(ks), GROUP):
        for slab in range(first, first + GROUP):
            for copy in loads(slab):
                copy.wait()
        scores = score_buf[first : first + GROUP].reshape(GROUP * SLAB, LABS).astype(jnp.float32)
        targets = target_buf[first : first + GROUP].reshape(GROUP * SLAB, LABS).astype(jnp.float32)
        half_tanh = 0.5 * jnp.tanh(0.5 * scores)
        gradient = half_tanh + (0.5 - targets)
        hessian = 0.25 - half_tanh * half_tanh
        hessian = hessian[:, :LANES] + hessian[:, LANES:]
        grad_high = gradient.astype(jnp.bfloat16)
        grad_low = (gradient - grad_high.astype(jnp.float32)).astype(jnp.bfloat16)
        hess_high = hessian.astype(jnp.bfloat16)
        hess_low = (hessian - hess_high.astype(jnp.float32)).astype(jnp.bfloat16)
        right = jnp.concatenate([grad_high, grad_low, hess_high, hess_low], axis=1)
        stats = lax.dot_general(left, right, NT, preferred_element_type=jnp.float32)
        for piece in range(GROUP * QUADS):
            at, lanes = piece % PIECES, slice(piece * LANES, (piece + 1) * LANES)
            out_ref = out_refs[(first * QUADS + piece) // PIECES]
            rows, row = slice(at * K, (at + 1) * K), slice(PIECES * K + at, PIECES * K + at + 1)
            sketch = stats[:K, lanes] * (1.0 / math.sqrt(L))
            curve = stats[K : K + 1, lanes] * (1.0 / L)
            for more_ref in more_refs:
                sketch += more_ref[rows, :]
                curve += more_ref[row, :]
            out_ref[rows, :] = sketch
            out_ref[row, :] = curve


def sketch_call(ks, scores, targets, signs_t, *more):
    slabs = 4 * len(ks)
    return pl.pallas_call(
        functools.partial(sketch_kernel, ks),
        in_specs=[
            pl.BlockSpec(memory_space=pl.ANY),
            pl.BlockSpec(memory_space=pl.ANY),
        ]
        + [pl.BlockSpec(memory_space=pltpu.VMEM)] * (1 + len(more)),
        out_specs=[pl.BlockSpec(memory_space=pltpu.VMEM)] * len(ks),
        out_shape=[jax.ShapeDtypeStruct((STAT_ROWS, LANES), jnp.float32)] * len(ks),
        scratch_shapes=[
            pltpu.VMEM((slabs, SLAB, LABS), jnp.bfloat16),
            pltpu.VMEM((slabs, SLAB, LABS), jnp.int32),
            pltpu.SemaphoreType.DMA((2, slabs)),
        ],
        compiler_params=pltpu.CompilerParams(vmem_limit_bytes=SKETCH_VMEM),
        cost_estimate=pl.CostEstimate(
            flops=2 * slabs * SLAB * 768 * 32,
            bytes_accessed=slabs * SLAB * LABS * 6,
            transcendentals=slabs * SLAB * LABS,
        ),
        name="sketch",
    )(scores, targets, signs_t, *more)


def split_terms(values, scales):
    terms = []
    for scale in scales:
        term = (values * scale).astype(F8).astype(jnp.float32)
        terms.append(term)
        values = values - term * (1.0 / scale)
    return terms


def weight_block(stats_ref, leaves_ref, chunk, write):
    leaf_iota = lax.broadcasted_iota(jnp.int32, (8, LANES), 0)
    zeros = jnp.zeros((K, LANES), jnp.float32)
    for piece in range(PIECES):
        leaf = leaves_ref[pl.ds(chunk * PIECES + piece, 1), :]
        sketch = stats_ref[piece * K : (piece + 1) * K, :]
        curve = stats_ref[PIECES * K + piece : PIECES * K + piece + 1, :]
        sketch = sketch.astype(jnp.bfloat16).astype(jnp.float32)
        curve = jnp.broadcast_to(curve, (8, LANES)).astype(jnp.bfloat16).astype(jnp.float32)
        masks = [jnp.broadcast_to(leaf == e, (K, LANES)) for e in range(LEAVES)]
        curve_mask = jnp.broadcast_to(leaf, (8, LANES)) == leaf_iota
        parts = [
            jnp.where(mask, term, zeros) for term in split_terms(sketch, SKETCH_SCALES) for mask in masks
        ]
        parts += [jnp.where(curve_mask, term, 0.0) for term in split_terms(curve, CURVE_SCALES)]
        parts.append(jnp.zeros((W_ROWS - 4 * TERM_ROWS - 16, LANES), jnp.float32))
        write(piece, jnp.concatenate(parts, axis=0).astype(F8))


def weight_kernel(ks, *refs):
    x = lax.axis_index("x").astype(jnp.int32)
    leaves_ref, out_ref = refs[-2:]
    for place, k in enumerate(ks):

        def write(piece, value, first=place * CHUNK):
            out_ref[:, first + piece * LANES : first + (piece + 1) * LANES] = value

        weight_block(refs[place], leaves_ref, x ^ k, write)


def weight_call(ks, stats, leaves):
    return pl.pallas_call(
        functools.partial(weight_kernel, ks),
        in_specs=[pl.BlockSpec(memory_space=pltpu.VMEM)] * (len(ks) + 1),
        out_specs=pl.BlockSpec(memory_space=pltpu.VMEM),
        out_shape=jax.ShapeDtypeStruct((W_ROWS, len(ks) * CHUNK), F8),
        compiler_params=pltpu.CompilerParams(vmem_limit_bytes=24 << 20),
        cost_estimate=pl.CostEstimate(flops=1_000_000, bytes_accessed=100_000, transcendentals=0),
        name="weights",
    )(*stats, leaves)


def count(codes, weights):
    codes = jnp.clip(codes, -1, OWN_BINS)
    pair = jnp.concatenate([codes, codes - 1], axis=0).astype(jnp.int8)
    one = jnp.ones(pair.shape, F8)
    zero = jnp.zeros(pair.shape, F8)
    onehot = jnp.concatenate(
        [jnp.where(pair == jnp.int8(b), one, zero) for b in range(0, OWN_BINS, 2)], axis=0
    )
    total = lax.dot_general(weights, onehot, NT, preferred_element_type=jnp.float32)
    sketch = sum(
        total[t * TERM_ROWS : (t + 1) * TERM_ROWS] * (1.0 / scale) for t, scale in enumerate(SKETCH_SCALES)
    )
    curve = sum(
        total[4 * TERM_ROWS + 8 * t : 4 * TERM_ROWS + 8 * t + 8] * (1.0 / scale)
        for t, scale in enumerate(CURVE_SCALES)
    )
    return jnp.concatenate(
        [sketch[:, :HALF], sketch[:, HALF:], curve[:LEAVES, :HALF], curve[:LEAVES, HALF:]], axis=0
    )


def first_bin(k, own):
    zl = lax.axis_index("zl").astype(jnp.int32)
    core = lax.axis_index("c").astype(jnp.int32)
    return OWN_BINS * (2 * (zl ^ k) + (core if own else 1 - core))


def block_bins(bins_ref, ks):
    x = lax.axis_index("x").astype(jnp.int32)
    return jnp.concatenate(
        [bins_ref[:, pl.ds(pl.multiple_of((x ^ k) * CHUNK, CHUNK), CHUNK)] for k in ks], axis=1
    )


def block_kernel(k, bins_ref, stats_ref, leaves_ref, *refs):
    out_ref, weights_ref = refs[-2:]
    weight_kernel((k,), stats_ref, leaves_ref, weights_ref)
    bins = block_bins(bins_ref, (k,))
    for to, own in ORDER:
        total = count(bins - first_bin(to, own), weights_ref[...])
        if len(refs) == 3:
            total += refs[0][4 * own + to]
        out_ref[4 * own + to] = total


def block_call(k, bins_t, stats, leaves, *before):
    return pl.pallas_call(
        functools.partial(block_kernel, k),
        in_specs=[pl.BlockSpec(memory_space=pltpu.VMEM)] * (3 + len(before)),
        out_specs=pl.BlockSpec(memory_space=pltpu.VMEM),
        out_shape=jax.ShapeDtypeStruct((8,) + PART, jnp.float32),
        scratch_shapes=[pltpu.VMEM((W_ROWS, CHUNK), F8)],
        compiler_params=pltpu.CompilerParams(vmem_limit_bytes=32 << 20),
        cost_estimate=pl.CostEstimate(flops=5_000_000_000, bytes_accessed=1_000_000, transcendentals=0),
        name="block",
    )(bins_t, stats, leaves, *before)


def other_kernel(ks, bins_ref, weights_ref, start_ref, out_ref):
    bins = block_bins(bins_ref, LAST)
    for place, k in enumerate(ks):
        out_ref[place] = start_ref[k] + count(bins - first_bin(k, False), weights_ref[...])


def other_call(ks, bins_t, weights, start):
    return pl.pallas_call(
        functools.partial(other_kernel, ks),
        in_specs=[pl.BlockSpec(memory_space=pltpu.VMEM)] * 3,
        out_specs=pl.BlockSpec(memory_space=pltpu.VMEM),
        out_shape=jax.ShapeDtypeStruct((len(ks),) + PART, jnp.float32),
        compiler_params=pltpu.CompilerParams(vmem_limit_bytes=32 << 20),
        cost_estimate=pl.CostEstimate(flops=OTHER_COST * len(ks), bytes_accessed=1000, transcendentals=0),
        name="other",
    )(bins_t, weights, start)


def hist_kernel(k, place, bins_ref, weights_ref, start_ref, swapped_ref, *refs):
    out_ref = refs[-1]
    bins = block_bins(bins_ref, LAST)
    total = start_ref[4 + k] + swapped_ref[place]
    for ref in refs[:-1]:
        total += ref[...]
    out_ref[...] = total + count(bins - first_bin(k, True), weights_ref[...])


def hist_call(k, bins_t, weights, start, swapped, place, *more):
    return pl.pallas_call(
        functools.partial(hist_kernel, k, place),
        in_specs=[pl.BlockSpec(memory_space=pltpu.VMEM)] * (4 + len(more)),
        out_specs=pl.BlockSpec(memory_space=pltpu.VMEM),
        out_shape=jax.ShapeDtypeStruct(PART, jnp.float32),
        compiler_params=pltpu.CompilerParams(vmem_limit_bytes=32 << 20),
        cost_estimate=pl.CostEstimate(flops=HIST_COST[k], bytes_accessed=1000, transcendentals=0),
        name="hist",
    )(bins_t, weights, start, swapped, *more)


def add_kernel(a_ref, b_ref, out_ref):
    out_ref[...] = a_ref[...] + b_ref[...]


def add_call(a, b, cost):
    return pl.pallas_call(
        add_kernel,
        in_specs=[pl.BlockSpec(memory_space=pltpu.VMEM)] * 2,
        out_specs=pl.BlockSpec(memory_space=pltpu.VMEM),
        out_shape=jax.ShapeDtypeStruct(PART, jnp.float32),
        compiler_params=pltpu.CompilerParams(vmem_limit_bytes=8 << 20),
        cost_estimate=pl.CostEstimate(flops=cost, bytes_accessed=1000, transcendentals=0),
        name="add",
    )(a, b)


def finish_kernel(a_ref, b_ref, out_ref):
    total = a_ref[...] + b_ref[...]
    for half in range(2):
        rows = []
        for e in range(LEAVES):
            first = half * TERM_ROWS + e * K
            rows.append(total[first : first + K])
            first = 2 * TERM_ROWS + half * LEAVES + e
            rows.append(total[first : first + 1])
        part = jnp.concatenate(rows, axis=0).T
        bins = OWN_BINS // 2
        out_ref[half * bins : (half + 1) * bins] = part.reshape(bins, FEATS, LEAVES * (K + 1))


def finish_call(parts):
    return pl.pallas_call(
        finish_kernel,
        out_shape=jax.ShapeDtypeStruct((OWN_BINS, FEATS, LEAVES * (K + 1)), jnp.float32),
        compiler_params=pltpu.CompilerParams(vmem_limit_bytes=8 << 20),
        name="finish",
    )(*parts)


def swap(value, axis, bit, size):
    return lax.ppermute(value, axis, [(i, i ^ bit) for i in range(size)])


def per_device(scores, targets, signs, bins, leaves):
    signs_t = signs.T
    bins_t = bins.T
    leaves2 = leaves.reshape(ROWS // LANES, LANES)

    (part,) = sketch_call((2,), scores, targets, signs_t)
    part, signs_t = lax.optimization_barrier((part, signs_t))
    first = swap(part, "x", 2, 4)
    parts = sketch_call((1, 3), scores, targets, signs_t)
    arrived = [swap(part, "x", k, 4) for k, part in zip((1, 3), parts)]
    (mine,) = sketch_call((0,), scores, targets, signs_t, first)
    mine = mine + (arrived[0] + arrived[1])
    arrived = [swap(mine, "y", k, 4) for k in (2, 1, 3)]
    mine = (mine + arrived[0]) + (arrived[1] + arrived[2])
    mine = mine + swap(mine, "zh", 1, 2)
    first = swap(mine, "x", 1, 4)
    last = [swap(mine, "x", k, 4) for k in LAST]
    start = block_call(0, bins_t, mine, leaves2)
    start = block_call(1, bins_t, first, leaves2, start)
    weights = weight_call(LAST, last, leaves2)

    far = swap(other_call((3,), bins_t, weights, start), "c", 1, 2)
    mid = other_call((2,), bins_t, weights, start)
    mid, start = lax.optimization_barrier((mid, start))
    mid = swap(mid, "c", 1, 2)
    part = hist_call(3, bins_t, weights, start, far, 0)
    part, start = lax.optimization_barrier((part, start))
    passed = swap(part, "zl", 1, 4)
    near = swap(other_call((1,), bins_t, weights, start), "c", 1, 2)
    part = hist_call(2, bins_t, weights, start, mid, 0)
    moved1 = swap(hist_call(1, bins_t, weights, start, near, 0), "zl", 1, 4)
    moved2 = swap(add_call(part, passed, ADD_COST), "zl", 2, 4)
    home = swap(other_call((0,), bins_t, weights, start), "c", 1, 2)
    part = hist_call(0, bins_t, weights, start, home, 0)
    return finish_call((add_call(part, moved1, ADD_COST), moved2))


def solution(mesh):
    fine = Mesh(mesh.devices.reshape(4, 2, 4, 4, 2), ("zl", "c", "y", "x", "zh"))
    row, lab = ("zl", "c"), ("y", "x", "zh")
    in_specs = (P(row, lab), P(row, lab), P(lab, None), P(row, lab), P(row))
    out_specs = P(row, lab, None)
    return jax.shard_map(
        per_device, mesh=fine, in_specs=in_specs, out_specs=out_specs, check_vma=False
    )
```

```python
import functools
import math

import jax
import jax.numpy as jnp
from jax import lax
from jax.experimental import pallas as pl
from jax.experimental.pallas import tpu as pltpu
from jax.sharding import Mesh, PartitionSpec as P

L = 8192
BINS = 256
K = 16
LEAVES = 4
ROWS = 8192
LABS = 256
FEATS = 16
SLAB = 512
LANES = 128
QUADS = SLAB // LANES
PIECES = 4 * QUADS
STAT_ROWS = PIECES * (K + 1)
F8 = jnp.float8_e4m3fn
NT = (((1,), (1,)), ((), ()))
SKETCH_SCALES = (4.0, 64.0, 2.0**24, 2.0**29)
CURVE_SCALES = (1024.0, 2.0**14)
TERM_ROWS = LEAVES * K
W_ROWS = 288
OWN_BINS = 32
CHUNK = 4 * SLAB
HALF = OWN_BINS * FEATS // 2
PART = (2 * LEAVES * (K + 1), HALF)
ORDER = tuple((k, own) for k in (3, 2, 1, 0) for own in (False, True))
OTHER_COST = 2_000_000_000
HIST_COST = (1000, 1000, 1000, 1000)
ADD_COST = 5_000_000_000
LAST = (3, 2)
GROUP = 4
SKETCH_VMEM = 51 << 20


def sketch_kernel(ks, scores_ref, targets_ref, signs_ref, *refs):
    more_refs, out_refs = refs[: -3 - len(ks)], refs[-3 - len(ks) : -3]
    score_buf, target_buf, sems = refs[-3:]
    x = lax.axis_index("x").astype(jnp.int32)

    def loads(slab):
        row = pl.multiple_of(((x ^ ks[slab // 4]) * 4 + slab % 4) * SLAB, SLAB)
        return (
            pltpu.make_async_copy(scores_ref.at[pl.ds(row, SLAB), :], score_buf.at[slab], sems.at[0, slab]),
            pltpu.make_async_copy(targets_ref.at[pl.ds(row, SLAB), :], target_buf.at[slab], sems.at[1, slab]),
        )

    for slab in range(4 * len(ks)):
        for copy in loads(slab):
            copy.start()
    sign_matrix = (2 * signs_ref[...] - 1).astype(jnp.bfloat16)
    left = jnp.concatenate(
        [
            jnp.concatenate([sign_matrix, sign_matrix, jnp.zeros((K, LABS), jnp.bfloat16)], axis=1),
            jnp.concatenate(
                [jnp.zeros((K, 2 * LABS), jnp.bfloat16), jnp.ones((K, LABS), jnp.bfloat16)], axis=1
            ),
        ],
        axis=0,
    )
    for first in range(0, 4 * len(ks), GROUP):
        for slab in range(first, first + GROUP):
            for copy in loads(slab):
                copy.wait()
        scores = score_buf[first : first + GROUP].reshape(GROUP * SLAB, LABS).astype(jnp.float32)
        targets = target_buf[first : first + GROUP].reshape(GROUP * SLAB, LABS).astype(jnp.float32)
        half_tanh = 0.5 * jnp.tanh(0.5 * scores)
        gradient = half_tanh + (0.5 - targets)
        hessian = 0.25 - half_tanh * half_tanh
        hessian = hessian[:, :LANES] + hessian[:, LANES:]
        grad_high = gradient.astype(jnp.bfloat16)
        grad_low = (gradient - grad_high.astype(jnp.float32)).astype(jnp.bfloat16)
        hess_high = hessian.astype(jnp.bfloat16)
        hess_low = (hessian - hess_high.astype(jnp.float32)).astype(jnp.bfloat16)
        right = jnp.concatenate([grad_high, grad_low, hess_high, hess_low], axis=1)
        stats = lax.dot_general(left, right, NT, preferred_element_type=jnp.float32)
        for piece in range(GROUP * QUADS):
            at, lanes = piece % PIECES, slice(piece * LANES, (piece + 1) * LANES)
            out_ref = out_refs[(first * QUADS + piece) // PIECES]
            rows, row = slice(at * K, (at + 1) * K), slice(PIECES * K + at, PIECES * K + at + 1)
            sketch = stats[:K, lanes] * (1.0 / math.sqrt(L))
            curve = stats[K : K + 1, lanes] * (1.0 / L)
            for more_ref in more_refs:
                sketch += more_ref[rows, :]
                curve += more_ref[row, :]
            out_ref[rows, :] = sketch
            out_ref[row, :] = curve


def sketch_call(ks, scores, targets, signs_t, *more):
    slabs = 4 * len(ks)
    return pl.pallas_call(
        functools.partial(sketch_kernel, ks),
        in_specs=[
            pl.BlockSpec(memory_space=pl.ANY),
            pl.BlockSpec(memory_space=pl.ANY),
        ]
        + [pl.BlockSpec(memory_space=pltpu.VMEM)] * (1 + len(more)),
        out_specs=[pl.BlockSpec(memory_space=pltpu.VMEM)] * len(ks),
        out_shape=[jax.ShapeDtypeStruct((STAT_ROWS, LANES), jnp.float32)] * len(ks),
        scratch_shapes=[
            pltpu.VMEM((slabs, SLAB, LABS), jnp.bfloat16),
            pltpu.VMEM((slabs, SLAB, LABS), jnp.int32),
            pltpu.SemaphoreType.DMA((2, slabs)),
        ],
        compiler_params=pltpu.CompilerParams(vmem_limit_bytes=SKETCH_VMEM),
        cost_estimate=pl.CostEstimate(
            flops=2 * slabs * SLAB * 768 * 32,
            bytes_accessed=slabs * SLAB * LABS * 6,
            transcendentals=slabs * SLAB * LABS,
        ),
        name="sketch",
    )(scores, targets, signs_t, *more)


def split_terms(values, scales):
    terms = []
    for scale in scales:
        term = (values * scale).astype(F8).astype(jnp.float32)
        terms.append(term)
        values = values - term * (1.0 / scale)
    return terms


def weight_block(stats_ref, leaves_ref, chunk, write):
    leaf_iota = lax.broadcasted_iota(jnp.int32, (8, LANES), 0)
    zeros = jnp.zeros((K, LANES), jnp.float32)
    for piece in range(PIECES):
        leaf = leaves_ref[pl.ds(chunk * PIECES + piece, 1), :]
        sketch = stats_ref[piece * K : (piece + 1) * K, :]
        curve = stats_ref[PIECES * K + piece : PIECES * K + piece + 1, :]
        sketch = sketch.astype(jnp.bfloat16).astype(jnp.float32)
        curve = jnp.broadcast_to(curve, (8, LANES)).astype(jnp.bfloat16).astype(jnp.float32)
        masks = [jnp.broadcast_to(leaf == e, (K, LANES)) for e in range(LEAVES)]
        curve_mask = jnp.broadcast_to(leaf, (8, LANES)) == leaf_iota
        parts = [
            jnp.where(mask, term, zeros) for term in split_terms(sketch, SKETCH_SCALES) for mask in masks
        ]
        parts += [jnp.where(curve_mask, term, 0.0) for term in split_terms(curve, CURVE_SCALES)]
        parts.append(jnp.zeros((W_ROWS - 4 * TERM_ROWS - 16, LANES), jnp.float32))
        write(piece, jnp.concatenate(parts, axis=0).astype(F8))


def weight_kernel(ks, *refs):
    x = lax.axis_index("x").astype(jnp.int32)
    leaves_ref, out_ref = refs[-2:]
    for place, k in enumerate(ks):

        def write(piece, value, first=place * CHUNK):
            out_ref[:, first + piece * LANES : first + (piece + 1) * LANES] = value

        weight_block(refs[place], leaves_ref, x ^ k, write)


def weight_call(ks, stats, leaves):
    return pl.pallas_call(
        functools.partial(weight_kernel, ks),
        in_specs=[pl.BlockSpec(memory_space=pltpu.VMEM)] * (len(ks) + 1),
        out_specs=pl.BlockSpec(memory_space=pltpu.VMEM),
        out_shape=jax.ShapeDtypeStruct((W_ROWS, len(ks) * CHUNK), F8),
        compiler_params=pltpu.CompilerParams(vmem_limit_bytes=24 << 20),
        cost_estimate=pl.CostEstimate(flops=1_000_000, bytes_accessed=100_000, transcendentals=0),
        name="weights",
    )(*stats, leaves)


def count(codes, weights):
    codes = jnp.clip(codes, -1, OWN_BINS)
    pair = jnp.concatenate([codes, codes - 1], axis=0).astype(jnp.int8)
    one = jnp.ones(pair.shape, F8)
    zero = jnp.zeros(pair.shape, F8)
    onehot = jnp.concatenate(
        [jnp.where(pair == jnp.int8(b), one, zero) for b in range(0, OWN_BINS, 2)], axis=0
    )
    total = lax.dot_general(weights, onehot, NT, preferred_element_type=jnp.float32)
    sketch = sum(
        total[t * TERM_ROWS : (t + 1) * TERM_ROWS] * (1.0 / scale) for t, scale in enumerate(SKETCH_SCALES)
    )
    curve = sum(
        total[4 * TERM_ROWS + 8 * t : 4 * TERM_ROWS + 8 * t + 8] * (1.0 / scale)
        for t, scale in enumerate(CURVE_SCALES)
    )
    return jnp.concatenate(
        [sketch[:, :HALF], sketch[:, HALF:], curve[:LEAVES, :HALF], curve[:LEAVES, HALF:]], axis=0
    )


def first_bin(k, own):
    zl = lax.axis_index("zl").astype(jnp.int32)
    core = lax.axis_index("c").astype(jnp.int32)
    return OWN_BINS * (2 * (zl ^ k) + (core if own else 1 - core))


def block_bins(bins_ref, ks):
    x = lax.axis_index("x").astype(jnp.int32)
    return jnp.concatenate(
        [bins_ref[:, pl.ds(pl.multiple_of((x ^ k) * CHUNK, CHUNK), CHUNK)] for k in ks], axis=1
    )


def block_kernel(k, bins_ref, stats_ref, leaves_ref, *refs):
    out_ref, weights_ref = refs[-2:]
    weight_kernel((k,), stats_ref, leaves_ref, weights_ref)
    bins = block_bins(bins_ref, (k,))
    for to, own in ORDER:
        total = count(bins - first_bin(to, own), weights_ref[...])
        if len(refs) == 3:
            total += refs[0][4 * own + to]
        out_ref[4 * own + to] = total


def block_call(k, bins_t, stats, leaves, *before):
    return pl.pallas_call(
        functools.partial(block_kernel, k),
        in_specs=[pl.BlockSpec(memory_space=pltpu.VMEM)] * (3 + len(before)),
        out_specs=pl.BlockSpec(memory_space=pltpu.VMEM),
        out_shape=jax.ShapeDtypeStruct((8,) + PART, jnp.float32),
        scratch_shapes=[pltpu.VMEM((W_ROWS, CHUNK), F8)],
        compiler_params=pltpu.CompilerParams(vmem_limit_bytes=32 << 20),
        cost_estimate=pl.CostEstimate(flops=5_000_000_000, bytes_accessed=1_000_000, transcendentals=0),
        name="block",
    )(bins_t, stats, leaves, *before)


def other_kernel(ks, bins_ref, weights_ref, start_ref, out_ref):
    bins = block_bins(bins_ref, LAST)
    for place, k in enumerate(ks):
        out_ref[place] = start_ref[k] + count(bins - first_bin(k, False), weights_ref[...])


def other_call(ks, bins_t, weights, start):
    return pl.pallas_call(
        functools.partial(other_kernel, ks),
        in_specs=[pl.BlockSpec(memory_space=pltpu.VMEM)] * 3,
        out_specs=pl.BlockSpec(memory_space=pltpu.VMEM),
        out_shape=jax.ShapeDtypeStruct((len(ks),) + PART, jnp.float32),
        compiler_params=pltpu.CompilerParams(vmem_limit_bytes=32 << 20),
        cost_estimate=pl.CostEstimate(flops=OTHER_COST * len(ks), bytes_accessed=1000, transcendentals=0),
        name="other",
    )(bins_t, weights, start)


def hist_kernel(k, place, bins_ref, weights_ref, start_ref, swapped_ref, *refs):
    out_ref = refs[-1]
    bins = block_bins(bins_ref, LAST)
    total = start_ref[4 + k] + swapped_ref[place]
    for ref in refs[:-1]:
        total += ref[...]
    out_ref[...] = total + count(bins - first_bin(k, True), weights_ref[...])


def hist_call(k, bins_t, weights, start, swapped, place, *more):
    return pl.pallas_call(
        functools.partial(hist_kernel, k, place),
        in_specs=[pl.BlockSpec(memory_space=pltpu.VMEM)] * (4 + len(more)),
        out_specs=pl.BlockSpec(memory_space=pltpu.VMEM),
        out_shape=jax.ShapeDtypeStruct(PART, jnp.float32),
        compiler_params=pltpu.CompilerParams(vmem_limit_bytes=32 << 20),
        cost_estimate=pl.CostEstimate(flops=HIST_COST[k], bytes_accessed=1000, transcendentals=0),
        name="hist",
    )(bins_t, weights, start, swapped, *more)


def add_kernel(a_ref, b_ref, out_ref):
    out_ref[...] = a_ref[...] + b_ref[...]


def add_call(a, b, cost):
    return pl.pallas_call(
        add_kernel,
        in_specs=[pl.BlockSpec(memory_space=pltpu.VMEM)] * 2,
        out_specs=pl.BlockSpec(memory_space=pltpu.VMEM),
        out_shape=jax.ShapeDtypeStruct(PART, jnp.float32),
        compiler_params=pltpu.CompilerParams(vmem_limit_bytes=8 << 20),
        cost_estimate=pl.CostEstimate(flops=cost, bytes_accessed=1000, transcendentals=0),
        name="add",
    )(a, b)


def finish_kernel(a_ref, b_ref, out_ref):
    total = a_ref[...] + b_ref[...]
    for half in range(2):
        rows = []
        for e in range(LEAVES):
            first = half * TERM_ROWS + e * K
            rows.append(total[first : first + K])
            first = 2 * TERM_ROWS + half * LEAVES + e
            rows.append(total[first : first + 1])
        part = jnp.concatenate(rows, axis=0).T
        bins = OWN_BINS // 2
        out_ref[half * bins : (half + 1) * bins] = part.reshape(bins, FEATS, LEAVES * (K + 1))


def finish_call(parts):
    return pl.pallas_call(
        finish_kernel,
        out_shape=jax.ShapeDtypeStruct((OWN_BINS, FEATS, LEAVES * (K + 1)), jnp.float32),
        compiler_params=pltpu.CompilerParams(vmem_limit_bytes=8 << 20),
        name="finish",
    )(*parts)


def swap(value, axis, bit, size):
    return lax.ppermute(value, axis, [(i, i ^ bit) for i in range(size)])


def per_device(scores, targets, signs, bins, leaves):
    signs_t = signs.T
    bins_t = bins.T
    leaves2 = leaves.reshape(ROWS // LANES, LANES)

    (part,) = sketch_call((2,), scores, targets, signs_t)
    part, signs_t = lax.optimization_barrier((part, signs_t))
    first = swap(part, "x", 2, 4)
    parts = sketch_call((1, 3), scores, targets, signs_t)
    arrived = [swap(part, "x", k, 4) for k, part in zip((1, 3), parts)]
    (mine,) = sketch_call((0,), scores, targets, signs_t, first)
    mine = mine + (arrived[0] + arrived[1])
    arrived = [swap(mine, "y", k, 4) for k in (1, 2, 3)]
    mine = (mine + arrived[0]) + (arrived[1] + arrived[2])
    mine = mine + swap(mine, "zh", 1, 2)
    first = swap(mine, "x", 1, 4)
    last = [swap(mine, "x", k, 4) for k in LAST]
    start = block_call(0, bins_t, mine, leaves2)
    start = block_call(1, bins_t, first, leaves2, start)
    weights = weight_call(LAST, last, leaves2)

    far = swap(other_call((3,), bins_t, weights, start), "c", 1, 2)
    mid = other_call((2,), bins_t, weights, start)
    mid, start = lax.optimization_barrier((mid, start))
    mid = swap(mid, "c", 1, 2)
    part = hist_call(3, bins_t, weights, start, far, 0)
    part, start = lax.optimization_barrier((part, start))
    passed = swap(part, "zl", 1, 4)
    near = swap(other_call((1,), bins_t, weights, start), "c", 1, 2)
    part = hist_call(2, bins_t, weights, start, mid, 0)
    moved1 = swap(hist_call(1, bins_t, weights, start, near, 0), "zl", 1, 4)
    moved2 = swap(add_call(part, passed, ADD_COST), "zl", 2, 4)
    home = swap(other_call((0,), bins_t, weights, start), "c", 1, 2)
    part = hist_call(0, bins_t, weights, start, home, 0)
    return finish_call((add_call(part, moved1, ADD_COST), moved2))


def solution(mesh):
    fine = Mesh(mesh.devices.reshape(4, 2, 4, 4, 2), ("zl", "c", "y", "x", "zh"))
    row, lab = ("zl", "c"), ("y", "x", "zh")
    in_specs = (P(row, lab), P(row, lab), P(lab, None), P(row, lab), P(row))
    out_specs = P(row, lab, None)
    return jax.shard_map(
        per_device, mesh=fine, in_specs=in_specs, out_specs=out_specs, check_vma=False
    )
```
